32 devices in a mesh: layer: 4 (over y, x), row: 2 (over core), col: 4 (over z).
Axes of the slice: x: 2, y: 2, z: 4, core: 2. Of those that a mesh axis runs over, the one named last changes fastest.
Arguments:
- l_blocks: bfloat16 [4, 8, 256, 256], P('layer', ('row', 'col')), may hold values from -3 to 3
- l_ids: int32 [4, 8], P('layer'), may hold values from 0 to 127, as said below
- u_blocks: bfloat16 [4, 8, 256, 256], P('layer', ('row', 'col')), may hold values from -3 to 3
- u_ids: int32 [4, 8], P('layer'), may hold values from 0 to 127, as said below
- inv_upper: bfloat16 [8, 256, 256], replicated, as said below
- inv_lower: bfloat16 [8, 256, 256], replicated, as said below
- row_order: int32 [16], replicated, may hold values from 0 to 15, as said below
- col_order: int32 [16], replicated, may hold values from 0 to 15, as said below
- front_in: float32 [16, 16, 256, 256], P('row', 'col', 'layer'), may hold values from -6 to 6
- leaf_lower: bfloat16 [32, 1024, 1024], P(('layer', 'row', 'col')), may hold values from -6 to 6
- leaf_upper: bfloat16 [32, 1024, 1024], P(('layer', 'row', 'col')), may hold values from -0.1875 to 0.1875
- leaf_front: bfloat16 [32, 1024, 1024], P(('layer', 'row', 'col')), may hold values from -6 to 6
Outputs:
- front_out: float32 [16, 16, 256, 256], P('row', 'col', 'layer')
- leaf_out: bfloat16 [32, 1024, 1024], P(('layer', 'row', 'col'))
The draws below stay inside these ranges and needn't reach their ends.
Inputs may be any that keep to these rules, and one draw needn't show every extreme that they name: `l_ids`: within a layer the ids are distinct; the entry at index r * 4 + c has i = row_order[r * 8 + p] for some p < 8. `u_ids`: within a layer the ids are distinct; the entry at index r * 4 + c has j = col_order[c * 4 + q] for some q < 4. `row_order`: A permutation of the tile rows. `col_order`: A permutation of the tile columns. `inv_upper`: each block is upper triangular with a positive diagonal. `inv_lower`: each block is lower triangular with a positive diagonal.
All inputs are finite; a program needn't handle non-finite values.
Results may differ from the reference program's by a relative error of at most 0.0095.
Values may be sent and summed in bfloat16 or wider, within the bound.
A program may use at most 128 MiB of HBM per device.

```python
import jax
import jax.numpy as jnp
from jax import lax

TB = 256
LF = 1024
KL = 1024
NT = 16
KB = 8
RPG = 8
CPG = 4
NBL = 8
LEAVES = 32
N_LAYER = 4
N_ROW = 2
N_COL = 4


def order_perm(key, salt):
    return jax.random.permutation(jax.random.fold_in(key, salt), NT).astype(jnp.int32)


def draw_row_order(key, part):
    return order_perm(key, 101)


def draw_col_order(key, part):
    return order_perm(key, 202)


def draw_l_ids(key, part):
    owned = order_perm(key, 101).reshape(N_ROW, RPG)
    keys = jax.random.split(jax.random.fold_in(key, 303), N_LAYER * N_ROW)
    picks = jax.vmap(lambda one: jax.random.permutation(one, RPG * KB)[:N_COL])(keys)
    picks = picks.reshape(N_LAYER, N_ROW, N_COL).astype(jnp.int32)
    grid_rows = jnp.arange(N_ROW, dtype=jnp.int32)[None, :, None]
    tile_row = owned[grid_rows, picks // KB]
    return (tile_row * KB + picks % KB).reshape(N_LAYER, N_ROW * N_COL).astype(jnp.int32)


def draw_u_ids(key, part):
    owned = order_perm(key, 202).reshape(N_COL, CPG)
    keys = jax.random.split(jax.random.fold_in(key, 404), N_LAYER * N_COL)
    picks = jax.vmap(lambda one: jax.random.permutation(one, CPG * KB)[:N_ROW])(keys)
    picks = picks.reshape(N_LAYER, N_COL, N_ROW).astype(jnp.int32)
    grid_cols = jnp.arange(N_COL, dtype=jnp.int32)[None, :, None]
    tile_col = owned[grid_cols, picks // KB]
    ids = picks % KB * NT + tile_col
    return ids.transpose(0, 2, 1).reshape(N_LAYER, N_ROW * N_COL).astype(jnp.int32)


def triangle(key, salt, upper_part):
    key_diag, key_off = jax.random.split(jax.random.fold_in(key, salt))
    diag = jax.random.uniform(key_diag, (KB, TB), minval=0.7, maxval=1.4)
    off = jnp.clip(jax.random.normal(key_off, (KB, TB, TB)), -4.0, 4.0) * (0.5 / TB ** 0.5)
    rows = jnp.arange(TB)[:, None]
    cols = jnp.arange(TB)[None, :]
    if upper_part:
        keep = cols > rows
    else:
        keep = cols < rows
    eye = (rows == cols).astype(jnp.float32)
    full = jnp.where(keep[None], off, 0.0) + diag[:, :, None] * eye[None]
    return full.astype(jnp.bfloat16)


def draw_inv_upper(key, part):
    return triangle(key, 505, True)


def draw_inv_lower(key, part):
    return triangle(key, 606, False)


def block_levels(rng, extent, shards, low, high):
    loudness, own = 1.0, jax.random.fold_in(rng, 6)
    for axis_at, shards_of in shards:
        heights = jnp.exp(jax.random.uniform(jax.random.fold_in(own, axis_at), (shards_of,), jnp.float32, low / len(shards), high / len(shards)))
        loudness = loudness * jnp.repeat(heights, extent[axis_at] // shards_of).reshape([-1 if axis == axis_at else 1 for axis in range(len(extent))])
    return loudness


def centred(key, extent, deviation, limit, cuts=(), kind=jnp.bfloat16):
    result = jax.random.normal(key, extent, jnp.float32) * deviation
    if len(cuts) > 0:
        result = block_levels(key, extent, cuts, -0.22, 0.18) * result
    return jnp.clip(result, min=-limit, max=limit).astype(kind)


def setup_inputs(seed: int = 0) -> dict:
    key_of = jax.random.split(jax.random.key(seed), 13)
    l_blocks = centred(key_of[0], (N_LAYER, NBL, TB, TB), 0.2, 3.0, ((0, 4), (1, 8)))
    l_ids = draw_l_ids(jax.random.fold_in(key_of[12], 71), 0)
    u_blocks = centred(key_of[2], (N_LAYER, NBL, TB, TB), 0.2, 3.0, ((0, 4), (1, 8)))
    u_ids = draw_u_ids(jax.random.fold_in(key_of[12], 71), 0)
    inv_upper = draw_inv_upper(jax.random.fold_in(key_of[12], 71), 0)
    inv_lower = draw_inv_lower(jax.random.fold_in(key_of[12], 71), 0)
    row_order = draw_row_order(jax.random.fold_in(key_of[12], 71), 0)
    col_order = draw_col_order(jax.random.fold_in(key_of[12], 71), 0)
    front_in = centred(key_of[8], (NT, NT, TB, TB), 1.0, 6.0, ((0, 2), (1, 4), (2, 4)), jnp.float32)
    leaf_lower = centred(key_of[9], (LEAVES, LF, KL), 1.0, 6.0, ((0, 32),))
    leaf_upper = centred(key_of[10], (LEAVES, KL, LF), KL ** -0.5, 0.1875, ((0, 32),))
    leaf_front = centred(key_of[11], (LEAVES, LF, LF), 1.0, 6.0, ((0, 32),))
    return {"l_blocks": l_blocks, "l_ids": l_ids, "u_blocks": u_blocks, "u_ids": u_ids, "inv_upper": inv_upper, "inv_lower": inv_lower, "row_order": row_order, "col_order": col_order, "front_in": front_in, "leaf_lower": leaf_lower, "leaf_upper": leaf_upper, "leaf_front": leaf_front}


def reference(l_blocks, l_ids, u_blocks, u_ids, inv_upper, inv_lower, row_order, col_order, front_in, leaf_lower, leaf_upper, leaf_front):
    highest = lax.Precision.HIGHEST
    schur = jnp.zeros((NT * TB, NT * TB), jnp.float32)
    for layer in range(N_LAYER):
        ids_low = l_ids[layer].astype(jnp.int32)
        ids_up = u_ids[layer].astype(jnp.int32)
        inv_u = inv_upper[ids_low % KB].astype(jnp.float32)
        lower = jnp.einsum("mab,mbc->mac", l_blocks[layer].astype(jnp.float32), inv_u, precision=highest).astype(jnp.bfloat16)
        inv_l = inv_lower[ids_up // NT].astype(jnp.float32)
        upper = jnp.einsum("mab,mbc->mac", inv_l, u_blocks[layer].astype(jnp.float32), precision=highest).astype(jnp.bfloat16)
        lpanel = jnp.zeros((NT * KB, TB, TB), jnp.bfloat16).at[ids_low].set(lower)
        lpanel = lpanel.reshape(NT, KB, TB, TB).transpose(0, 2, 1, 3).reshape(NT * TB, KB * TB)
        upanel = jnp.zeros((KB * NT, TB, TB), jnp.bfloat16).at[ids_up].set(upper)
        upanel = upanel.reshape(KB, NT, TB, TB).transpose(0, 2, 1, 3).reshape(KB * TB, NT * TB)
        schur = schur + jnp.dot(lpanel.astype(jnp.float32), upanel.astype(jnp.float32), precision=highest)
    tiles = schur.reshape(NT, TB, NT, TB).transpose(0, 2, 1, 3)
    tiles = tiles[row_order.astype(jnp.int32)][:, col_order.astype(jnp.int32)]
    front_out = front_in - tiles
    update = jnp.einsum("nab,nbc->nac", leaf_lower.astype(jnp.float32), leaf_upper.astype(jnp.float32), precision=highest)
    leaf_out = (leaf_front.astype(jnp.float32) - update).astype(jnp.bfloat16)
    return front_out, leaf_out
```

```python
import functools

import jax
import jax.numpy as jnp
from jax import lax
from jax.experimental import pallas as pl
from jax.experimental.pallas import tpu as pltpu
from jax.sharding import PartitionSpec as P

MESH = pl.DeviceIdType.MESH
LEAF_ROWS = 512
LEAF_COLS = 256


def exchange(
    sizes,
    l_ids_sm, u_ids_sm, l_ids_hbm, u_ids_hbm, l_hbm, u_hbm, inv_u_hbm, inv_l_hbm,
    front_hbm, ll_hbm, lu_hbm, lf_hbm,
    low_all, up_all, l_ids_all, u_ids_all, front_v, leaf_v,
    l_v, u_v, inv_u, inv_l, lower, upper, ll, lu, lf,
    loc, low_recv, low_send, line_send, up_recv, up_send, up_fwd, ids_recv, ids_send,
):
    n_layer, n_row, n_col, tiles_side = sizes
    lay = lax.axis_index("layer")
    row = lax.axis_index("row")
    col = lax.axis_index("col")
    panels = inv_u.shape[0]
    high = low_all.shape[2]

    def layer_at(t):
        return lax.rem(lay + t, n_layer)

    def row_at(t):
        return lax.rem(row + t, n_row)

    local = [
        (inv_u_hbm, inv_u), (l_hbm.at[0, 0], l_v), (inv_l_hbm, inv_l), (u_hbm.at[0, 0], u_v),
        (ll_hbm.at[0], ll), (lu_hbm.at[0], lu), (lf_hbm.at[0], lf), (front_hbm, front_v),
        (l_ids_hbm, l_ids_all.at[lay]), (u_ids_hbm, u_ids_all.at[lay]),
    ]
    local = [pltpu.make_async_copy(src, dst, loc.at[i]) for i, (src, dst) in enumerate(local)]
    for copy in local:
        copy.start()

    barrier = pltpu.get_barrier_semaphore()

    def greet(device):
        pl.semaphore_signal(barrier, inc=1, device_id=device, device_id_type=MESH)

    for t in range(1, n_layer):
        greet({"layer": layer_at(t)})
    for t in range(1, n_row):
        greet({"row": row_at(t)})

    @pl.when(col + 1 < n_col)
    def _():
        greet({"col": col + 1})

    @pl.when(col > 0)
    def _():
        greet({"col": col - 1})

    def low_copy(src, s, l, sem, device):
        return pltpu.make_async_remote_copy(
            src_ref=src, dst_ref=low_all.at[s, l], send_sem=sem, recv_sem=low_recv.at[s, l],
            device_id=device, device_id_type=MESH)

    def up_copy(src, l, sem, device):
        return pltpu.make_async_remote_copy(
            src_ref=src, dst_ref=up_all.at[row, l], send_sem=sem, recv_sem=up_recv.at[row, l],
            device_id=device, device_id_type=MESH)

    def low_rows(l):
        return lower.at[pl.ds(pl.multiple_of(l * high, high), high)]

    def right(s, l):
        return low_copy(low_all.at[s, l], s, l, line_send.at[0, s, l], {"col": col + 1})

    def left(s, l):
        return low_copy(low_all.at[s, l], s, l, line_send.at[1, s, l], {"col": col - 1})

    def plane(t):
        l = layer_at(t)
        return low_copy(low_rows(l), col, lay, low_send.at[l], {"layer": l})

    def up_plane(t):
        l = layer_at(t)
        return up_copy(upper, lay, up_send.at[l], {"layer": l})

    def up_row(l, t):
        r = row_at(t)
        return up_copy(up_all.at[row, l], l, up_fwd.at[r, l], {"row": r})

    def ids_copy(which, src, dst, t):
        l = layer_at(t)
        return pltpu.make_async_remote_copy(
            src_ref=src, dst_ref=dst.at[lay], send_sem=ids_send.at[which, l],
            recv_sem=ids_recv.at[which, lay], device_id={"layer": l}, device_id_type=MESH)

    def low_arrived(s, l):
        low_copy(low_all.at[s, l], s, l, low_send.at[0], {"layer": layer_at(1)}).wait_recv()

    def leaf(first, last):
        per = ll.shape[0] // LEAF_ROWS

        def body(i, carry):
            rows = pl.ds(pl.multiple_of(lax.rem(i, per) * LEAF_ROWS, LEAF_ROWS), LEAF_ROWS)
            cols = pl.ds(pl.multiple_of((i // per) * LEAF_COLS, LEAF_COLS), LEAF_COLS)
            update = jnp.dot(ll[rows, :], lu[:, cols], preferred_element_type=jnp.float32)
            leaf_v[rows, cols] = (lf[rows, cols].astype(jnp.float32) - update).astype(leaf_v.dtype)
            return carry

        lax.fori_loop(first, last, body, 0)

    n_leaf = (ll.shape[0] // LEAF_ROWS) * (lu.shape[1] // LEAF_COLS)
    place = row * n_col + col

    local[0].wait()
    local[1].wait()
    lower[...] = jnp.dot(
        l_v[...], inv_u[l_ids_sm[0, place] % panels], preferred_element_type=jnp.float32
    ).astype(lower.dtype)
    low_all[col, lay] = low_rows(lay)[...]

    on_line = (col + 1 < n_col).astype(jnp.int32) + (col > 0).astype(jnp.int32)
    pl.semaphore_wait(barrier, n_layer - 1 + n_row - 1 + on_line)

    for t in range(1, n_layer):
        plane(t).start()

    def pass_on(s, l, go_right, go_left):
        if go_right:
            @pl.when(col + 1 < n_col)
            def _():
                right(s, l).start()
        if go_left:
            @pl.when(col > 0)
            def _():
                left(s, l).start()

    pass_on(col, lay, True, True)

    local[2].wait()
    local[3].wait()
    upper[...] = jnp.dot(
        inv_l[u_ids_sm[0, place] // tiles_side], u_v[...], preferred_element_type=jnp.float32
    ).astype(upper.dtype)
    up_all[row, lay] = upper[...]
    for t in range(1, n_layer):
        up_plane(t).start()
    for t in range(1, n_row):
        up_row(lay, t).start()
    for t in range(1, n_layer):
        ids_copy(0, l_ids_hbm, l_ids_all, t).start()
        ids_copy(1, u_ids_hbm, u_ids_all, t).start()

    for copy in local[4:]:
        copy.wait()

    for t in range(1, n_layer):
        l = layer_at(t)
        low_arrived(col, l)
        pass_on(col, l, True, True)
    leaf(0, n_leaf // 4)

    for d in range(1, n_col):
        for t in range(n_layer):
            l = layer_at(t)

            @pl.when(col - d >= 0)
            def _():
                low_arrived(col - d, l)
                pass_on(col - d, l, True, False)

            @pl.when(col + d < n_col)
            def _():
                low_arrived(col + d, l)
                pass_on(col + d, l, False, True)

        if d == 1:
            leaf(n_leaf // 4, n_leaf)
        if d == max(1, n_col - 2):
            for t in range(1, n_layer):
                l = layer_at(t)
                up_copy(upper, l, up_send.at[l], {"layer": l}).wait_recv()
                for u in range(1, n_row):
                    up_row(l, u).start()

    for t in range(1, n_row):
        for l in range(n_layer):
            r = row_at(t)
            pltpu.make_async_remote_copy(
                src_ref=upper, dst_ref=up_all.at[r, l], send_sem=up_fwd.at[r, l],
                recv_sem=up_recv.at[r, l], device_id={"row": r}, device_id_type=MESH).wait_recv()
            up_row(l, t).wait_send()
    for t in range(1, n_layer):
        plane(t).wait_send()
        up_plane(t).wait_send()
        l = layer_at(t)
        for which, src, dst in ((0, l_ids_hbm, l_ids_all), (1, u_ids_hbm, u_ids_all)):
            ids_copy(which, src, dst, t).wait_send()
            pltpu.make_async_remote_copy(
                src_ref=src, dst_ref=dst.at[l], send_sem=ids_send.at[which, l],
                recv_sem=ids_recv.at[which, l], device_id={"layer": l},
                device_id_type=MESH).wait_recv()
    for d in range(n_col):
        for l in range(n_layer):
            @pl.when((col - d >= 0) & (col + 1 < n_col))
            def _():
                right(col - d, l).wait_send()

            @pl.when((col + d < n_col) & (col > 0))
            def _():
                left(col + d, l).wait_send()


def finish(
    sizes,
    l_ids, u_ids, row_order, col_order, low_all, up_all, front_v, leaf_v,
    front_out, leaf_out, acc, sem,
):
    n_layer, n_row, n_col, tiles_side, panels = sizes
    row = lax.axis_index("row")
    col = lax.axis_index("col")
    rows_owned, cols_owned = acc.shape[0], acc.shape[1]
    leaf_copy = pltpu.make_async_copy(leaf_v, leaf_out.at[0], sem.at[0])
    leaf_copy.start()
    acc[...] = front_v[...]

    def find(order, start, count, value):
        at = jnp.int32(0)
        for a in range(count):
            at = jnp.where(order[start + a] == value, jnp.int32(a), at)
        return at

    for l in range(n_layer):
        for m2 in range(n_row):
            uid = u_ids[l, 0, m2 * n_col + col]
            for m in range(n_col):
                lid = l_ids[l, 0, row * n_col + m]

                @pl.when(lid % panels == uid // tiles_side)
                def _():
                    p = find(row_order, row * rows_owned, rows_owned, lid // panels)
                    q = find(col_order, col * cols_owned, cols_owned, uid % tiles_side)
                    acc[p, q] = acc[p, q] - jnp.dot(
                        low_all[m, l], up_all[m2, l], preferred_element_type=jnp.float32)

    front_copy = pltpu.make_async_copy(acc, front_out, sem.at[1])
    front_copy.start()
    front_copy.wait()
    leaf_copy.wait()


def shards(
    sizes,
    l_blocks, l_ids, u_blocks, u_ids, inv_upper, inv_lower, row_order, col_order,
    front_in, leaf_lower, leaf_upper, leaf_front,
):
    n_layer, n_row, n_col = sizes
    tile = l_blocks.shape[-1]
    high = front_in.shape[2]
    n_ids = l_ids.shape[1]
    tiles_side = row_order.shape[0]
    bf16, i32 = jnp.bfloat16, jnp.int32
    vmem = pl.BlockSpec(memory_space=pltpu.VMEM)
    smem = pl.BlockSpec(memory_space=pltpu.SMEM)
    any_ = pl.BlockSpec(memory_space=pl.ANY)
    hbm = pl.BlockSpec(memory_space=pltpu.HBM)
    dma = pltpu.SemaphoreType.DMA
    leaf_shape = leaf_front.shape[1:]
    low_all, up_all, l_all, u_all, front_v, leaf_v = pl.pallas_call(
        functools.partial(exchange, (n_layer, n_row, n_col, tiles_side)),
        name="exchange",
        out_shape=(
            pltpu.VMEM((n_col, n_layer, high, tile), bf16),
            pltpu.VMEM((n_row, n_layer, tile, tile), bf16),
            jax.ShapeDtypeStruct((n_layer, 1, n_ids), i32),
            jax.ShapeDtypeStruct((n_layer, 1, n_ids), i32),
            pltpu.VMEM(front_in.shape, front_in.dtype),
            pltpu.VMEM(leaf_shape, bf16),
        ),
        in_specs=[smem, smem] + [hbm] * 10,
        out_specs=(vmem, vmem, any_, any_, vmem, vmem),
        scratch_shapes=[
            pltpu.VMEM((tile, tile), bf16),
            pltpu.VMEM((tile, tile), bf16),
            pltpu.VMEM(inv_upper.shape, bf16),
            pltpu.VMEM(inv_lower.shape, bf16),
            pltpu.VMEM((tile, tile), bf16),
            pltpu.VMEM((tile, tile), bf16),
            pltpu.VMEM(leaf_lower.shape[1:], bf16),
            pltpu.VMEM(leaf_upper.shape[1:], bf16),
            pltpu.VMEM(leaf_shape, bf16),
            dma((10,)),
            dma((n_col, n_layer)),
            dma((n_layer,)),
            dma((2, n_col, n_layer)),
            dma((n_row, n_layer)),
            dma((n_layer,)),
            dma((n_row, n_layer)),
            dma((2, n_layer)),
            dma((2, n_layer)),
        ],
        compiler_params=pltpu.CompilerParams(
            collective_id=0, has_side_effects=True, vmem_limit_bytes=28 * 2**20),
    )(l_ids, u_ids, l_ids, u_ids, l_blocks, u_blocks, inv_upper, inv_lower,
      front_in, leaf_lower, leaf_upper, leaf_front)
    return pl.pallas_call(
        functools.partial(finish, (n_layer, n_row, n_col, tiles_side, inv_upper.shape[0])),
        name="finish",
        out_shape=(
            jax.ShapeDtypeStruct(front_in.shape, front_in.dtype),
            jax.ShapeDtypeStruct(leaf_front.shape, bf16),
        ),
        in_specs=[smem] * 4 + [vmem] * 4,
        out_specs=(any_, any_),
        scratch_shapes=[pltpu.VMEM(front_in.shape, front_in.dtype), dma((2,))],
        compiler_params=pltpu.CompilerParams(vmem_limit_bytes=28 * 2**20),
    )(l_all, u_all, row_order, col_order, low_all, up_all, front_v, leaf_v)


def solution(mesh):
    sizes = (mesh.shape["layer"], mesh.shape["row"], mesh.shape["col"])
    leaf = P(("layer", "row", "col"), None, None)
    return jax.shard_map(
        functools.partial(shards, sizes),
        mesh=mesh,
        in_specs=(
            P("layer", ("row", "col"), None, None),
            P("layer", None),
            P("layer", ("row", "col"), None, None),
            P("layer", None),
            P(),
            P(),
            P(),
            P(),
            P("row", "col", "layer", None),
            leaf,
            leaf,
            leaf,
        ),
        out_specs=(P("row", "col", "layer", None), leaf),
        check_vma=False,
    )
```

```python
import functools

import jax
import jax.numpy as jnp
from jax import lax
from jax.experimental import pallas as pl
from jax.experimental.pallas import tpu as pltpu
from jax.sharding import PartitionSpec as P

MESH = pl.DeviceIdType.MESH
LEAF_ROWS = 512
LEAF_COLS = 256


def exchange(
    sizes,
    l_ids_sm, u_ids_sm, l_ids_hbm, u_ids_hbm, l_hbm, u_hbm, inv_u_hbm, inv_l_hbm,
    front_hbm, ll_hbm, lu_hbm, lf_hbm,
    low_all, up_all, l_ids_all, u_ids_all, front_v, leaf_v,
    l_v, u_v, inv_u, inv_l, lower, upper, ll, lu, lf,
    loc, low_recv, low_send, line_send, up_recv, up_send, up_fwd, ids_recv, ids_send,
):
    n_layer, n_row, n_col, tiles_side = sizes
    lay = lax.axis_index("layer")
    row = lax.axis_index("row")
    col = lax.axis_index("col")
    panels = inv_u.shape[0]
    high = low_all.shape[2]

    def layer_at(t):
        return lax.rem(lay + t, n_layer)

    def row_at(t):
        return lax.rem(row + t, n_row)

    local = [
        (inv_u_hbm, inv_u), (l_hbm.at[0, 0], l_v), (inv_l_hbm, inv_l), (u_hbm.at[0, 0], u_v),
        (ll_hbm.at[0], ll), (lu_hbm.at[0], lu), (lf_hbm.at[0], lf), (front_hbm, front_v),
        (l_ids_hbm, l_ids_all.at[lay]), (u_ids_hbm, u_ids_all.at[lay]),
    ]
    local = [pltpu.make_async_copy(src, dst, loc.at[i]) for i, (src, dst) in enumerate(local)]
    for copy in local:
        copy.start()

    barrier = pltpu.get_barrier_semaphore()

    def greet(device):
        pl.semaphore_signal(barrier, inc=1, device_id=device, device_id_type=MESH)

    for t in range(1, n_layer):
        greet({"layer": layer_at(t)})
    for t in range(1, n_row):
        greet({"row": row_at(t)})

    @pl.when(col + 1 < n_col)
    def _():
        greet({"col": col + 1})

    @pl.when(col > 0)
    def _():
        greet({"col": col - 1})

    def low_copy(src, s, l, sem, device):
        return pltpu.make_async_remote_copy(
            src_ref=src, dst_ref=low_all.at[s, l], send_sem=sem, recv_sem=low_recv.at[s, l],
            device_id=device, device_id_type=MESH)

    def up_copy(src, l, sem, device):
        return pltpu.make_async_remote_copy(
            src_ref=src, dst_ref=up_all.at[row, l], send_sem=sem, recv_sem=up_recv.at[row, l],
            device_id=device, device_id_type=MESH)

    def low_rows(l):
        return lower.at[pl.ds(pl.multiple_of(l * high, high), high)]

    def right(s, l):
        return low_copy(low_all.at[s, l], s, l, line_send.at[0, s, l], {"col": col + 1})

    def left(s, l):
        return low_copy(low_all.at[s, l], s, l, line_send.at[1, s, l], {"col": col - 1})

    def plane(t):
        l = layer_at(t)
        return low_copy(low_rows(l), col, lay, low_send.at[l], {"layer": l})

    def up_plane(t):
        l = layer_at(t)
        return up_copy(upper, lay, up_send.at[l], {"layer": l})

    def up_row(l, t):
        r = row_at(t)
        return up_copy(up_all.at[row, l], l, up_fwd.at[r, l], {"row": r})

    def ids_copy(which, src, dst, t):
        l = layer_at(t)
        return pltpu.make_async_remote_copy(
            src_ref=src, dst_ref=dst.at[lay], send_sem=ids_send.at[which, l],
            recv_sem=ids_recv.at[which, lay], device_id={"layer": l}, device_id_type=MESH)

    def low_arrived(s, l):
        low_copy(low_all.at[s, l], s, l, low_send.at[0], {"layer": layer_at(1)}).wait_recv()

    def leaf(first, last):
        per = ll.shape[0] // LEAF_ROWS

        def body(i, carry):
            rows = pl.ds(pl.multiple_of(lax.rem(i, per) * LEAF_ROWS, LEAF_ROWS), LEAF_ROWS)
            cols = pl.ds(pl.multiple_of((i // per) * LEAF_COLS, LEAF_COLS), LEAF_COLS)
            update = jnp.dot(ll[rows, :], lu[:, cols], preferred_element_type=jnp.float32)
            leaf_v[rows, cols] = (lf[rows, cols].astype(jnp.float32) - update).astype(leaf_v.dtype)
            return carry

        lax.fori_loop(first, last, body, 0)

    n_leaf = (ll.shape[0] // LEAF_ROWS) * (lu.shape[1] // LEAF_COLS)
    place = row * n_col + col

    local[0].wait()
    local[1].wait()
    lower[...] = jnp.dot(
        l_v[...], inv_u[l_ids_sm[0, place] % panels], preferred_element_type=jnp.float32
    ).astype(lower.dtype)
    low_all[col, lay] = low_rows(lay)[...]

    on_line = (col + 1 < n_col).astype(jnp.int32) + (col > 0).astype(jnp.int32)
    pl.semaphore_wait(barrier, n_layer - 1 + n_row - 1 + on_line)

    for t in range(1, n_layer):
        plane(t).start()

    def pass_on(s, l, go_right, go_left):
        if go_right:
            @pl.when(col + 1 < n_col)
            def _():
                right(s, l).start()
        if go_left:
            @pl.when(col > 0)
            def _():
                left(s, l).start()

    pass_on(col, lay, True, True)

    local[2].wait()
    local[3].wait()
    upper[...] = jnp.dot(
        inv_l[u_ids_sm[0, place] // tiles_side], u_v[...], preferred_element_type=jnp.float32
    ).astype(upper.dtype)
    up_all[row, lay] = upper[...]
    for t in range(1, n_layer):
        up_plane(t).start()
    for t in range(1, n_row):
        up_row(lay, t).start()
    for t in range(1, n_layer):
        ids_copy(0, l_ids_hbm, l_ids_all, t).start()
        ids_copy(1, u_ids_hbm, u_ids_all, t).start()

    for copy in local[4:]:
        copy.wait()

    for t in range(1, n_layer):
        l = layer_at(t)
        low_arrived(col, l)
        pass_on(col, l, True, True)
    leaf(0, n_leaf // 4)

    for d in range(1, n_col):
        for t in range(n_layer):
            l = layer_at(t)

            @pl.when(col - d >= 0)
            def _():
                low_arrived(col - d, l)
                pass_on(col - d, l, True, False)

            @pl.when(col + d < n_col)
            def _():
                low_arrived(col + d, l)
                pass_on(col + d, l, False, True)

        if d == 1:
            leaf(n_leaf // 4, n_leaf)
        if d == max(1, n_col - 2):
            for t in range(1, n_layer):
                l = layer_at(t)
                up_copy(upper, l, up_send.at[l], {"layer": l}).wait_recv()
                for u in range(1, n_row):
                    up_row(l, u).start()

    for t in range(1, n_row):
        for l in range(n_layer):
            r = row_at(t)
            pltpu.make_async_remote_copy(
                src_ref=upper, dst_ref=up_all.at[r, l], send_sem=up_fwd.at[r, l],
                recv_sem=up_recv.at[r, l], device_id={"row": r}, device_id_type=MESH).wait_recv()
            up_row(l, t).wait_send()
    for t in range(1, n_layer):
        plane(t).wait_send()
        up_plane(t).wait_send()
        l = layer_at(t)
        for which, src, dst in ((0, l_ids_hbm, l_ids_all), (1, u_ids_hbm, u_ids_all)):
            ids_copy(which, src, dst, t).wait_send()
            pltpu.make_async_remote_copy(
                src_ref=src, dst_ref=dst.at[l], send_sem=ids_send.at[which, l],
                recv_sem=ids_recv.at[which, l], device_id={"layer": l},
                device_id_type=MESH).wait_recv()
    for d in range(n_col):
        for l in range(n_layer):
            @pl.when((col - d >= 0) & (col + 1 < n_col))
            def _():
                right(col - d, l).wait_send()

            @pl.when((col + d < n_col) & (col > 0))
            def _():
                left(col + d, l).wait_send()


def finish(
    sizes,
    l_ids, u_ids, row_order, col_order, low_all, up_all, front_v, leaf_v,
    front_out, leaf_out, acc, sem,
):
    n_layer, n_row, n_col, tiles_side, panels = sizes
    row = lax.axis_index("row")
    col = lax.axis_index("col")
    rows_owned, cols_owned = acc.shape[0], acc.shape[1]
    leaf_copy = pltpu.make_async_copy(leaf_v, leaf_out.at[0], sem.at[0])
    leaf_copy.start()
    acc[...] = front_v[...]

    def find(order, start, count, value):
        at = jnp.int32(0)
        for a in range(count):
            at = jnp.where(order[start + a] == value, jnp.int32(a), at)
        return at

    for l in range(n_layer):
        for m2 in range(n_row):
            uid = u_ids[l, 0, m2 * n_col + col]
            for m in range(n_col):
                lid = l_ids[l, 0, row * n_col + m]

                @pl.when(lid % panels == uid // tiles_side)
                def _():
                    p = find(row_order, row * rows_owned, rows_owned, lid // panels)
                    q = find(col_order, col * cols_owned, cols_owned, uid % tiles_side)
                    acc[p, q] = acc[p, q] - jnp.dot(
                        low_all[m, l], up_all[m2, l], preferred_element_type=jnp.float32)

    front_copy = pltpu.make_async_copy(acc, front_out, sem.at[1])
    front_copy.start()
    front_copy.wait()
    leaf_copy.wait()


def shards(
    sizes,
    l_blocks, l_ids, u_blocks, u_ids, inv_upper, inv_lower, row_order, col_order,
    front_in, leaf_lower, leaf_upper, leaf_front,
):
    n_layer, n_row, n_col = sizes
    tile = l_blocks.shape[-1]
    high = front_in.shape[2]
    n_ids = l_ids.shape[1]
    tiles_side = row_order.shape[0]
    bf16, i32 = jnp.bfloat16, jnp.int32
    vmem = pl.BlockSpec(memory_space=pltpu.VMEM)
    smem = pl.BlockSpec(memory_space=pltpu.SMEM)
    any_ = pl.BlockSpec(memory_space=pl.ANY)
    hbm = pl.BlockSpec(memory_space=pltpu.HBM)
    dma = pltpu.SemaphoreType.DMA
    leaf_shape = leaf_front.shape[1:]
    low_all, up_all, l_all, u_all, front_v, leaf_v = pl.pallas_call(
        functools.partial(exchange, (n_layer, n_row, n_col, tiles_side)),
        name="exchange",
        out_shape=(
            pltpu.VMEM((n_col, n_layer, high, tile), bf16),
            pltpu.VMEM((n_row, n_layer, tile, tile), bf16),
            jax.ShapeDtypeStruct((n_layer, 1, n_ids), i32),
            jax.ShapeDtypeStruct((n_layer, 1, n_ids), i32),
            pltpu.VMEM(front_in.shape, front_in.dtype),
            pltpu.VMEM(leaf_shape, bf16),
        ),
        in_specs=[smem, smem] + [hbm] * 10,
        out_specs=(vmem, vmem, any_, any_, vmem, vmem),
        scratch_shapes=[
            pltpu.VMEM((tile, tile), bf16),
            pltpu.VMEM((tile, tile), bf16),
            pltpu.VMEM(inv_upper.shape, bf16),
            pltpu.VMEM(inv_lower.shape, bf16),
            pltpu.VMEM((tile, tile), bf16),
            pltpu.VMEM((tile, tile), bf16),
            pltpu.VMEM(leaf_lower.shape[1:], bf16),
            pltpu.VMEM(leaf_upper.shape[1:], bf16),
            pltpu.VMEM(leaf_shape, bf16),
            dma((10,)),
            dma((n_col, n_layer)),
            dma((n_layer,)),
            dma((2, n_col, n_layer)),
            dma((n_row, n_layer)),
            dma((n_layer,)),
            dma((n_row, n_layer)),
            dma((2, n_layer)),
            dma((2, n_layer)),
        ],
        compiler_params=pltpu.CompilerParams(
            collective_id=0, has_side_effects=True, vmem_limit_bytes=28 * 2**20),
    )(l_ids, u_ids, *(pltpu.with_memory_space_constraint(x, pltpu.HBM) for x in (
        l_ids, u_ids, l_blocks, u_blocks, inv_upper, inv_lower, front_in, leaf_lower,
        leaf_upper, leaf_front)))
    return pl.pallas_call(
        functools.partial(finish, (n_layer, n_row, n_col, tiles_side, inv_upper.shape[0])),
        name="finish",
        out_shape=(
            jax.ShapeDtypeStruct(front_in.shape, front_in.dtype),
            jax.ShapeDtypeStruct(leaf_front.shape, bf16),
        ),
        in_specs=[smem] * 4 + [vmem] * 4,
        out_specs=(any_, any_),
        scratch_shapes=[pltpu.VMEM(front_in.shape, front_in.dtype), dma((2,))],
        compiler_params=pltpu.CompilerParams(vmem_limit_bytes=28 * 2**20),
    )(l_all, u_all, row_order, col_order, low_all, up_all, front_v, leaf_v)


def solution(mesh):
    sizes = (mesh.shape["layer"], mesh.shape["row"], mesh.shape["col"])
    leaf = P(("layer", "row", "col"), None, None)
    return jax.shard_map(
        functools.partial(shards, sizes),
        mesh=mesh,
        in_specs=(
            P("layer", ("row", "col"), None, None),
            P("layer", None),
            P("layer", ("row", "col"), None, None),
            P("layer", None),
            P(),
            P(),
            P(),
            P(),
            P("row", "col", "layer", None),
            leaf,
            leaf,
            leaf,
        ),
        out_specs=(P("row", "col", "layer", None), leaf),
        check_vma=False,
    )
```

```python
import functools

import jax
import jax.numpy as jnp
from jax import lax
from jax.experimental import pallas as pl
from jax.experimental.pallas import tpu as pltpu
from jax.sharding import PartitionSpec as P

MESH = pl.DeviceIdType.MESH
LEAF_ROWS = 512
LEAF_COLS = 256


def exchange(
    sizes,
    l_ids_sm, u_ids_sm, l_ids_hbm, u_ids_hbm, l_hbm, u_hbm, inv_u_hbm, inv_l_hbm,
    front_hbm, ll_hbm, lu_hbm, lf_hbm,
    low_all, up_all, l_ids_all, u_ids_all, front_v, leaf_v,
    l_v, u_v, inv_u, inv_l, lower, upper, ll, lu, lf,
    loc, low_recv, low_send, line_send, up_recv, up_send, up_fwd, ids_recv, ids_send,
):
    n_layer, n_row, n_col, tiles_side = sizes
    lay = lax.axis_index("layer")
    row = lax.axis_index("row")
    col = lax.axis_index("col")
    panels = inv_u.shape[0]
    high = low_all.shape[2]

    def layer_at(t):
        return lax.rem(lay + t, n_layer)

    def row_at(t):
        return lax.rem(row + t, n_row)

    local = [
        (inv_u_hbm, inv_u), (l_hbm.at[0, 0], l_v), (inv_l_hbm, inv_l), (u_hbm.at[0, 0], u_v),
        (ll_hbm.at[0], ll), (lu_hbm.at[0], lu), (lf_hbm.at[0], lf), (front_hbm, front_v),
        (l_ids_hbm, l_ids_all.at[lay]), (u_ids_hbm, u_ids_all.at[lay]),
    ]
    local = [pltpu.make_async_copy(src, dst, loc.at[i]) for i, (src, dst) in enumerate(local)]
    for copy in local[:4]:
        copy.start()

    barrier = pltpu.get_barrier_semaphore()

    def greet(device):
        pl.semaphore_signal(barrier, inc=1, device_id=device, device_id_type=MESH)

    for t in range(1, n_layer):
        greet({"layer": layer_at(t)})
    for t in range(1, n_row):
        greet({"row": row_at(t)})

    @pl.when(col + 1 < n_col)
    def _():
        greet({"col": col + 1})

    @pl.when(col > 0)
    def _():
        greet({"col": col - 1})

    def low_copy(src, s, l, sem, device):
        return pltpu.make_async_remote_copy(
            src_ref=src, dst_ref=low_all.at[s, l], send_sem=sem, recv_sem=low_recv.at[s, l],
            device_id=device, device_id_type=MESH)

    def up_copy(src, l, sem, device):
        return pltpu.make_async_remote_copy(
            src_ref=src, dst_ref=up_all.at[row, l], send_sem=sem, recv_sem=up_recv.at[row, l],
            device_id=device, device_id_type=MESH)

    def low_rows(l):
        return lower.at[pl.ds(pl.multiple_of(l * high, high), high)]

    def right(s, l):
        return low_copy(low_all.at[s, l], s, l, line_send.at[0, s, l], {"col": col + 1})

    def left(s, l):
        return low_copy(low_all.at[s, l], s, l, line_send.at[1, s, l], {"col": col - 1})

    def plane(t):
        l = layer_at(t)
        return low_copy(low_rows(l), col, lay, low_send.at[l], {"layer": l})

    def up_plane(t):
        l = layer_at(t)
        return up_copy(upper, lay, up_send.at[l], {"layer": l})

    def up_row(l, t):
        r = row_at(t)
        return up_copy(up_all.at[row, l], l, up_fwd.at[r, l], {"row": r})

    def ids_copy(which, src, dst, t):
        l = layer_at(t)
        return pltpu.make_async_remote_copy(
            src_ref=src, dst_ref=dst.at[lay], send_sem=ids_send.at[which, l],
            recv_sem=ids_recv.at[which, lay], device_id={"layer": l}, device_id_type=MESH)

    def low_arrived(s, l):
        low_copy(low_all.at[s, l], s, l, low_send.at[0], {"layer": layer_at(1)}).wait_recv()

    def leaf(first, last):
        per = ll.shape[0] // LEAF_ROWS

        def body(i, carry):
            rows = pl.ds(pl.multiple_of(lax.rem(i, per) * LEAF_ROWS, LEAF_ROWS), LEAF_ROWS)
            cols = pl.ds(pl.multiple_of((i // per) * LEAF_COLS, LEAF_COLS), LEAF_COLS)
            update = jnp.dot(ll[rows, :], lu[:, cols], preferred_element_type=jnp.float32)
            leaf_v[rows, cols] = (lf[rows, cols].astype(jnp.float32) - update).astype(leaf_v.dtype)
            return carry

        lax.fori_loop(first, last, body, 0)

    n_leaf = (ll.shape[0] // LEAF_ROWS) * (lu.shape[1] // LEAF_COLS)
    place = row * n_col + col

    local[0].wait()
    local[1].wait()
    lower[...] = jnp.dot(
        l_v[...], inv_u[l_ids_sm[0, place] % panels], preferred_element_type=jnp.float32
    ).astype(lower.dtype)
    low_all[col, lay] = low_rows(lay)[...]

    on_line = (col + 1 < n_col).astype(jnp.int32) + (col > 0).astype(jnp.int32)
    pl.semaphore_wait(barrier, n_layer - 1 + n_row - 1 + on_line)

    for t in range(1, n_layer):
        plane(t).start()

    def pass_on(s, l, go_right, go_left):
        if go_right:
            @pl.when(col + 1 < n_col)
            def _():
                right(s, l).start()
        if go_left:
            @pl.when(col > 0)
            def _():
                left(s, l).start()

    pass_on(col, lay, True, True)

    local[2].wait()
    local[3].wait()
    upper[...] = jnp.dot(
        inv_l[u_ids_sm[0, place] // tiles_side], u_v[...], preferred_element_type=jnp.float32
    ).astype(upper.dtype)
    up_all[row, lay] = upper[...]
    for t in range(1, n_layer):
        up_plane(t).start()
    for t in range(1, n_row):
        up_row(lay, t).start()
    for t in range(1, n_layer):
        ids_copy(0, l_ids_hbm, l_ids_all, t).start()
        ids_copy(1, u_ids_hbm, u_ids_all, t).start()

    for copy in local[4:]:
        copy.start()

    for t in range(1, n_layer):
        l = layer_at(t)
        low_arrived(col, l)
        pass_on(col, l, True, True)

    for d in range(1, n_col):
        for t in range(n_layer):
            l = layer_at(t)

            @pl.when(col - d >= 0)
            def _():
                low_arrived(col - d, l)
                pass_on(col - d, l, True, False)

            @pl.when(col + d < n_col)
            def _():
                low_arrived(col + d, l)
                pass_on(col + d, l, False, True)

            step = (d - 1) * n_layer + t
            if step == 0:
                for copy in local[4:]:
                    copy.wait()
            if step < n_leaf:
                last = n_leaf if step == (n_col - 1) * n_layer - 1 else step + 1
                leaf(step, last)

        if d == max(1, n_col - 2):
            for t in range(1, n_layer):
                l = layer_at(t)
                up_copy(upper, l, up_send.at[l], {"layer": l}).wait_recv()
                for u in range(1, n_row):
                    up_row(l, u).start()

    for t in range(1, n_row):
        for l in range(n_layer):
            r = row_at(t)
            pltpu.make_async_remote_copy(
                src_ref=upper, dst_ref=up_all.at[r, l], send_sem=up_fwd.at[r, l],
                recv_sem=up_recv.at[r, l], device_id={"row": r}, device_id_type=MESH).wait_recv()
            up_row(l, t).wait_send()
    for t in range(1, n_layer):
        plane(t).wait_send()
        up_plane(t).wait_send()
        l = layer_at(t)
        for which, src, dst in ((0, l_ids_hbm, l_ids_all), (1, u_ids_hbm, u_ids_all)):
            ids_copy(which, src, dst, t).wait_send()
            pltpu.make_async_remote_copy(
                src_ref=src, dst_ref=dst.at[l], send_sem=ids_send.at[which, l],
                recv_sem=ids_recv.at[which, l], device_id={"layer": l},
                device_id_type=MESH).wait_recv()
    for d in range(n_col):
        for l in range(n_layer):
            @pl.when((col - d >= 0) & (col + 1 < n_col))
            def _():
                right(col - d, l).wait_send()

            @pl.when((col + d < n_col) & (col > 0))
            def _():
                left(col + d, l).wait_send()


def finish(
    sizes,
    l_ids, u_ids, row_order, col_order, low_all, up_all, front_v, leaf_v,
    front_out, leaf_out, acc, sem,
):
    n_layer, n_row, n_col, tiles_side, panels = sizes
    row = lax.axis_index("row")
    col = lax.axis_index("col")
    rows_owned, cols_owned = acc.shape[0], acc.shape[1]
    leaf_copy = pltpu.make_async_copy(leaf_v, leaf_out.at[0], sem.at[0])
    leaf_copy.start()
    acc[...] = front_v[...]

    def find(order, start, count, value):
        at = jnp.int32(0)
        for a in range(count):
            at = jnp.where(order[start + a] == value, jnp.int32(a), at)
        return at

    for l in range(n_layer):
        for m2 in range(n_row):
            uid = u_ids[l, 0, m2 * n_col + col]
            for m in range(n_col):
                lid = l_ids[l, 0, row * n_col + m]

                @pl.when(lid % panels == uid // tiles_side)
                def _():
                    p = find(row_order, row * rows_owned, rows_owned, lid // panels)
                    q = find(col_order, col * cols_owned, cols_owned, uid % tiles_side)
                    acc[p, q] = acc[p, q] - jnp.dot(
                        low_all[m, l], up_all[m2, l], preferred_element_type=jnp.float32)

    front_copy = pltpu.make_async_copy(acc, front_out, sem.at[1])
    front_copy.start()
    front_copy.wait()
    leaf_copy.wait()


def shards(
    sizes,
    l_blocks, l_ids, u_blocks, u_ids, inv_upper, inv_lower, row_order, col_order,
    front_in, leaf_lower, leaf_upper, leaf_front,
):
    n_layer, n_row, n_col = sizes
    tile = l_blocks.shape[-1]
    high = front_in.shape[2]
    n_ids = l_ids.shape[1]
    tiles_side = row_order.shape[0]
    bf16, i32 = jnp.bfloat16, jnp.int32
    vmem = pl.BlockSpec(memory_space=pltpu.VMEM)
    smem = pl.BlockSpec(memory_space=pltpu.SMEM)
    any_ = pl.BlockSpec(memory_space=pl.ANY)
    hbm = pl.BlockSpec(memory_space=pltpu.HBM)
    dma = pltpu.SemaphoreType.DMA
    leaf_shape = leaf_front.shape[1:]
    low_all, up_all, l_all, u_all, front_v, leaf_v = pl.pallas_call(
        functools.partial(exchange, (n_layer, n_row, n_col, tiles_side)),
        name="exchange",
        out_shape=(
            pltpu.VMEM((n_col, n_layer, high, tile), bf16),
            pltpu.VMEM((n_row, n_layer, tile, tile), bf16),
            jax.ShapeDtypeStruct((n_layer, 1, n_ids), i32),
            jax.ShapeDtypeStruct((n_layer, 1, n_ids), i32),
            pltpu.VMEM(front_in.shape, front_in.dtype),
            pltpu.VMEM(leaf_shape, bf16),
        ),
        in_specs=[smem, smem] + [hbm] * 10,
        out_specs=(vmem, vmem, any_, any_, vmem, vmem),
        scratch_shapes=[
            pltpu.VMEM((tile, tile), bf16),
            pltpu.VMEM((tile, tile), bf16),
            pltpu.VMEM(inv_upper.shape, bf16),
            pltpu.VMEM(inv_lower.shape, bf16),
            pltpu.VMEM((tile, tile), bf16),
            pltpu.VMEM((tile, tile), bf16),
            pltpu.VMEM(leaf_lower.shape[1:], bf16),
            pltpu.VMEM(leaf_upper.shape[1:], bf16),
            pltpu.VMEM(leaf_shape, bf16),
            dma((10,)),
            dma((n_col, n_layer)),
            dma((n_layer,)),
            dma((2, n_col, n_layer)),
            dma((n_row, n_layer)),
            dma((n_layer,)),
            dma((n_row, n_layer)),
            dma((2, n_layer)),
            dma((2, n_layer)),
        ],
        compiler_params=pltpu.CompilerParams(
            collective_id=0, has_side_effects=True, vmem_limit_bytes=28 * 2**20),
    )(l_ids, u_ids, *(pltpu.with_memory_space_constraint(x, pltpu.HBM) for x in (
        l_ids, u_ids, l_blocks, u_blocks, inv_upper, inv_lower, front_in, leaf_lower,
        leaf_upper, leaf_front)))
    return pl.pallas_call(
        functools.partial(finish, (n_layer, n_row, n_col, tiles_side, inv_upper.shape[0])),
        name="finish",
        out_shape=(
            jax.ShapeDtypeStruct(front_in.shape, front_in.dtype),
            jax.ShapeDtypeStruct(leaf_front.shape, bf16),
        ),
        in_specs=[smem] * 4 + [vmem] * 4,
        out_specs=(any_, any_),
        scratch_shapes=[pltpu.VMEM(front_in.shape, front_in.dtype), dma((2,))],
        compiler_params=pltpu.CompilerParams(vmem_limit_bytes=28 * 2**20),
    )(l_all, u_all, row_order, col_order, low_all, up_all, front_v, leaf_v)


def solution(mesh):
    sizes = (mesh.shape["layer"], mesh.shape["row"], mesh.shape["col"])
    leaf = P(("layer", "row", "col"), None, None)
    return jax.shard_map(
        functools.partial(shards, sizes),
        mesh=mesh,
        in_specs=(
            P("layer", ("row", "col"), None, None),
            P("layer", None),
            P("layer", ("row", "col"), None, None),
            P("layer", None),
            P(),
            P(),
            P(),
            P(),
            P("row", "col", "layer", None),
            leaf,
            leaf,
            leaf,
        ),
        out_specs=(P("row", "col", "layer", None), leaf),
        check_vma=False,
    )
```

```python
import functools

import jax
import jax.numpy as jnp
from jax import lax
from jax.experimental import pallas as pl
from jax.experimental.pallas import tpu as pltpu
from jax.sharding import PartitionSpec as P

MESH = pl.DeviceIdType.MESH
LEAF_ROWS = 512
LEAF_COLS = 256


def exchange(
    sizes,
    l_ids_sm, u_ids_sm, l_ids_hbm, u_ids_hbm, l_hbm, u_hbm, inv_u_hbm, inv_l_hbm,
    front_hbm, ll_hbm, lu_hbm, lf_hbm,
    low_all, up_all, l_ids_all, u_ids_all, front_v, leaf_v,
    l_v, u_v, inv_u, inv_l, lower, upper, ll, lu, lf,
    loc, low_recv, low_send, line_send, up_recv, up_send, up_fwd, ids_recv, ids_send,
):
    n_layer, n_row, n_col, tiles_side = sizes
    lay = lax.axis_index("layer")
    row = lax.axis_index("row")
    col = lax.axis_index("col")
    panels = inv_u.shape[0]
    high = low_all.shape[2]

    def layer_at(t):
        return lax.rem(lay + t, n_layer)

    def row_at(t):
        return lax.rem(row + t, n_row)

    local = [
        (inv_u_hbm, inv_u), (l_hbm.at[0, 0], l_v), (inv_l_hbm, inv_l), (u_hbm.at[0, 0], u_v),
        (ll_hbm.at[0], ll), (lu_hbm.at[0], lu), (lf_hbm.at[0], lf), (front_hbm, front_v),
        (l_ids_hbm, l_ids_all.at[lay]), (u_ids_hbm, u_ids_all.at[lay]),
    ]
    local = [pltpu.make_async_copy(src, dst, loc.at[i]) for i, (src, dst) in enumerate(local)]
    for copy in local[:4]:
        copy.start()

    barrier = pltpu.get_barrier_semaphore()

    def greet(device):
        pl.semaphore_signal(barrier, inc=1, device_id=device, device_id_type=MESH)

    for t in range(1, n_layer):
        greet({"layer": layer_at(t)})
    for t in range(1, n_row):
        greet({"row": row_at(t)})

    @pl.when(col + 1 < n_col)
    def _():
        greet({"col": col + 1})

    @pl.when(col > 0)
    def _():
        greet({"col": col - 1})

    def low_copy(src, s, l, sem, device):
        return pltpu.make_async_remote_copy(
            src_ref=src, dst_ref=low_all.at[s, l], send_sem=sem, recv_sem=low_recv.at[s, l],
            device_id=device, device_id_type=MESH)

    def up_copy(src, l, sem, device):
        return pltpu.make_async_remote_copy(
            src_ref=src, dst_ref=up_all.at[row, l], send_sem=sem, recv_sem=up_recv.at[row, l],
            device_id=device, device_id_type=MESH)

    def low_rows(l):
        return lower.at[pl.ds(pl.multiple_of(l * high, high), high)]

    def right(s, l):
        return low_copy(low_all.at[s, l], s, l, line_send.at[0, s, l], {"col": col + 1})

    def left(s, l):
        return low_copy(low_all.at[s, l], s, l, line_send.at[1, s, l], {"col": col - 1})

    def plane(t):
        l = layer_at(t)
        return low_copy(low_rows(l), col, lay, low_send.at[l], {"layer": l})

    def up_plane(t):
        l = layer_at(t)
        return up_copy(upper, lay, up_send.at[l], {"layer": l})

    def up_row(l, t):
        r = row_at(t)
        return up_copy(up_all.at[row, l], l, up_fwd.at[r, l], {"row": r})

    def ids_copy(which, src, dst, t):
        l = layer_at(t)
        return pltpu.make_async_remote_copy(
            src_ref=src, dst_ref=dst.at[lay], send_sem=ids_send.at[which, l],
            recv_sem=ids_recv.at[which, lay], device_id={"layer": l}, device_id_type=MESH)

    def low_arrived(s, l):
        low_copy(low_all.at[s, l], s, l, low_send.at[0], {"layer": layer_at(1)}).wait_recv()

    def leaf(i):
        per = ll.shape[0] // LEAF_ROWS
        rows = pl.ds(pl.multiple_of(lax.rem(i, per) * LEAF_ROWS, LEAF_ROWS), LEAF_ROWS)
        cols = pl.ds(pl.multiple_of((i // per) * LEAF_COLS, LEAF_COLS), LEAF_COLS)
        update = jnp.dot(ll[rows, :], lu[:, cols], preferred_element_type=jnp.float32)
        leaf_v[rows, cols] = (lf[rows, cols].astype(jnp.float32) - update).astype(leaf_v.dtype)

    n_leaf = (ll.shape[0] // LEAF_ROWS) * (lu.shape[1] // LEAF_COLS)
    place = row * n_col + col

    local[0].wait()
    local[1].wait()
    lower[...] = jnp.dot(
        l_v[...], inv_u[l_ids_sm[0, place] % panels], preferred_element_type=jnp.float32
    ).astype(lower.dtype)
    low_all[col, lay] = low_rows(lay)[...]

    on_line = (col + 1 < n_col).astype(jnp.int32) + (col > 0).astype(jnp.int32)
    pl.semaphore_wait(barrier, n_layer - 1 + n_row - 1 + on_line)

    for t in range(1, n_layer):
        plane(t).start()

    def pass_on(s, l, go_right, go_left):
        if go_right:
            @pl.when(col + 1 < n_col)
            def _():
                right(s, l).start()
        if go_left:
            @pl.when(col > 0)
            def _():
                left(s, l).start()

    pass_on(col, lay, True, True)

    local[2].wait()
    local[3].wait()
    upper[...] = jnp.dot(
        inv_l[u_ids_sm[0, place] // tiles_side], u_v[...], preferred_element_type=jnp.float32
    ).astype(upper.dtype)
    up_all[row, lay] = upper[...]
    for t in range(1, n_row):
        up_row(lay, t).start()
    for copy in local[4:]:
        copy.start()

    for t in range(1, n_layer):
        l = layer_at(t)
        low_arrived(col, l)
        pass_on(col, l, True, True)
    for t in range(1, n_layer):
        up_plane(t).start()
    for t in range(1, n_layer):
        ids_copy(0, l_ids_hbm, l_ids_all, t).start()
        ids_copy(1, u_ids_hbm, u_ids_all, t).start()

    up_round = max(1, n_col - 2)
    n_steps = (n_col - 1) * n_layer

    def line_step(step, carry):
        d = step // n_layer + 1
        t = lax.rem(step, n_layer)
        l = layer_at(t)

        @pl.when(col - d >= 0)
        def _():
            low_arrived(col - d, l)
            pass_on(col - d, l, True, False)

        @pl.when(col + d < n_col)
        def _():
            low_arrived(col + d, l)
            pass_on(col + d, l, False, True)

        @pl.when((d == up_round) & (t > 0))
        def _():
            up_copy(upper, l, up_send.at[l], {"layer": l}).wait_recv()
            for u in range(1, n_row):
                up_row(l, u).start()

        @pl.when(step < n_leaf)
        def _():
            leaf(step)

        return carry

    for copy in local[4:]:
        copy.wait()
    lax.fori_loop(0, n_steps, line_step, 0)
    for i in range(n_steps, n_leaf):
        leaf(i)

    for t in range(1, n_row):
        for l in range(n_layer):
            r = row_at(t)
            pltpu.make_async_remote_copy(
                src_ref=upper, dst_ref=up_all.at[r, l], send_sem=up_fwd.at[r, l],
                recv_sem=up_recv.at[r, l], device_id={"row": r}, device_id_type=MESH).wait_recv()
            up_row(l, t).wait_send()
    for t in range(1, n_layer):
        plane(t).wait_send()
        up_plane(t).wait_send()
        l = layer_at(t)
        for which, src, dst in ((0, l_ids_hbm, l_ids_all), (1, u_ids_hbm, u_ids_all)):
            ids_copy(which, src, dst, t).wait_send()
            pltpu.make_async_remote_copy(
                src_ref=src, dst_ref=dst.at[l], send_sem=ids_send.at[which, l],
                recv_sem=ids_recv.at[which, l], device_id={"layer": l},
                device_id_type=MESH).wait_recv()
    for d in range(n_col):
        for l in range(n_layer):
            @pl.when((col - d >= 0) & (col + 1 < n_col))
            def _():
                right(col - d, l).wait_send()

            @pl.when((col + d < n_col) & (col > 0))
            def _():
                left(col + d, l).wait_send()


def finish(
    sizes,
    l_ids, u_ids, row_order, col_order, low_all, up_all, front_v, leaf_v,
    front_out, leaf_out, acc, sem,
):
    n_layer, n_row, n_col, tiles_side, panels = sizes
    row = lax.axis_index("row")
    col = lax.axis_index("col")
    rows_owned, cols_owned = acc.shape[0], acc.shape[1]
    leaf_copy = pltpu.make_async_copy(leaf_v, leaf_out.at[0], sem.at[0])
    leaf_copy.start()
    acc[...] = front_v[...]

    def find(order, start, count, value):
        at = jnp.int32(0)
        for a in range(count):
            at = jnp.where(order[start + a] == value, jnp.int32(a), at)
        return at

    for l in range(n_layer):
        for m2 in range(n_row):
            uid = u_ids[l, 0, m2 * n_col + col]
            for m in range(n_col):
                lid = l_ids[l, 0, row * n_col + m]

                @pl.when(lid % panels == uid // tiles_side)
                def _():
                    p = find(row_order, row * rows_owned, rows_owned, lid // panels)
                    q = find(col_order, col * cols_owned, cols_owned, uid % tiles_side)
                    acc[p, q] = acc[p, q] - jnp.dot(
                        low_all[m, l], up_all[m2, l], preferred_element_type=jnp.float32)

    front_copy = pltpu.make_async_copy(acc, front_out, sem.at[1])
    front_copy.start()
    front_copy.wait()
    leaf_copy.wait()


def shards(
    sizes,
    l_blocks, l_ids, u_blocks, u_ids, inv_upper, inv_lower, row_order, col_order,
    front_in, leaf_lower, leaf_upper, leaf_front,
):
    n_layer, n_row, n_col = sizes
    tile = l_blocks.shape[-1]
    high = front_in.shape[2]
    n_ids = l_ids.shape[1]
    tiles_side = row_order.shape[0]
    bf16, i32 = jnp.bfloat16, jnp.int32
    vmem = pl.BlockSpec(memory_space=pltpu.VMEM)
    smem = pl.BlockSpec(memory_space=pltpu.SMEM)
    any_ = pl.BlockSpec(memory_space=pl.ANY)
    hbm = pl.BlockSpec(memory_space=pltpu.HBM)
    dma = pltpu.SemaphoreType.DMA
    leaf_shape = leaf_front.shape[1:]
    low_all, up_all, l_all, u_all, front_v, leaf_v = pl.pallas_call(
        functools.partial(exchange, (n_layer, n_row, n_col, tiles_side)),
        name="exchange",
        out_shape=(
            pltpu.VMEM((n_col, n_layer, high, tile), bf16),
            pltpu.VMEM((n_row, n_layer, tile, tile), bf16),
            jax.ShapeDtypeStruct((n_layer, 1, n_ids), i32),
            jax.ShapeDtypeStruct((n_layer, 1, n_ids), i32),
            pltpu.VMEM(front_in.shape, front_in.dtype),
            pltpu.VMEM(leaf_shape, bf16),
        ),
        in_specs=[smem, smem] + [hbm] * 10,
        out_specs=(vmem, vmem, any_, any_, vmem, vmem),
        scratch_shapes=[
            pltpu.VMEM((tile, tile), bf16),
            pltpu.VMEM((tile, tile), bf16),
            pltpu.VMEM(inv_upper.shape, bf16),
            pltpu.VMEM(inv_lower.shape, bf16),
            pltpu.VMEM((tile, tile), bf16),
            pltpu.VMEM((tile, tile), bf16),
            pltpu.VMEM(leaf_lower.shape[1:], bf16),
            pltpu.VMEM(leaf_upper.shape[1:], bf16),
            pltpu.VMEM(leaf_shape, bf16),
            dma((10,)),
            dma((n_col, n_layer)),
            dma((n_layer,)),
            dma((2, n_col, n_layer)),
            dma((n_row, n_layer)),
            dma((n_layer,)),
            dma((n_row, n_layer)),
            dma((2, n_layer)),
            dma((2, n_layer)),
        ],
        compiler_params=pltpu.CompilerParams(
            collective_id=0, has_side_effects=True, vmem_limit_bytes=28 * 2**20),
    )(l_ids, u_ids, *(pltpu.with_memory_space_constraint(x, pltpu.HBM) for x in (
        l_ids, u_ids, l_blocks, u_blocks, inv_upper, inv_lower, front_in, leaf_lower,
        leaf_upper, leaf_front)))
    return pl.pallas_call(
        functools.partial(finish, (n_layer, n_row, n_col, tiles_side, inv_upper.shape[0])),
        name="finish",
        out_shape=(
            jax.ShapeDtypeStruct(front_in.shape, front_in.dtype),
            jax.ShapeDtypeStruct(leaf_front.shape, bf16),
        ),
        in_specs=[smem] * 4 + [vmem] * 4,
        out_specs=(any_, any_),
        scratch_shapes=[pltpu.VMEM(front_in.shape, front_in.dtype), dma((2,))],
        compiler_params=pltpu.CompilerParams(vmem_limit_bytes=28 * 2**20),
    )(l_all, u_all, row_order, col_order, low_all, up_all, front_v, leaf_v)


def solution(mesh):
    sizes = (mesh.shape["layer"], mesh.shape["row"], mesh.shape["col"])
    leaf = P(("layer", "row", "col"), None, None)
    return jax.shard_map(
        functools.partial(shards, sizes),
        mesh=mesh,
        in_specs=(
            P("layer", ("row", "col"), None, None),
            P("layer", None),
            P("layer", ("row", "col"), None, None),
            P("layer", None),
            P(),
            P(),
            P(),
            P(),
            P("row", "col", "layer", None),
            leaf,
            leaf,
            leaf,
        ),
        out_specs=(P("row", "col", "layer", None), leaf),
        check_vma=False,
    )
```

```python
import functools

import jax
import jax.numpy as jnp
from jax import lax
from jax.experimental import pallas as pl
from jax.experimental.pallas import tpu as pltpu
from jax.sharding import PartitionSpec as P

MESH = pl.DeviceIdType.MESH
LEAF_ROWS = 512
LEAF_COLS = 256


def exchange(
    sizes,
    l_ids_sm, u_ids_sm, l_ids_hbm, u_ids_hbm, l_hbm, u_hbm, inv_u_hbm, inv_l_hbm,
    front_hbm, ll_hbm, lu_hbm, lf_hbm,
    low_all, up_all, l_ids_all, u_ids_all, front_v, leaf_v,
    l_v, u_v, inv_u, inv_l, lower, upper, ll, lu, lf,
    loc, low_recv, low_send, line_send, up_recv, up_send, up_fwd, ids_recv, ids_send,
):
    n_layer, n_row, n_col, tiles_side = sizes
    lay = lax.axis_index("layer")
    row = lax.axis_index("row")
    col = lax.axis_index("col")
    panels = inv_u.shape[0]
    high = low_all.shape[2]

    def layer_at(t):
        return lax.rem(lay + t, n_layer)

    def row_at(t):
        return lax.rem(row + t, n_row)

    local = [
        (inv_u_hbm, inv_u), (l_hbm.at[0, 0], l_v), (inv_l_hbm, inv_l), (u_hbm.at[0, 0], u_v),
        (ll_hbm.at[0], ll), (lu_hbm.at[0], lu), (lf_hbm.at[0], lf), (front_hbm, front_v),
        (l_ids_hbm, l_ids_all.at[lay]), (u_ids_hbm, u_ids_all.at[lay]),
    ]
    local = [pltpu.make_async_copy(src, dst, loc.at[i]) for i, (src, dst) in enumerate(local)]
    for copy in local[:4]:
        copy.start()

    barrier = pltpu.get_barrier_semaphore()

    def greet(device):
        pl.semaphore_signal(barrier, inc=1, device_id=device, device_id_type=MESH)

    for t in range(1, n_layer):
        greet({"layer": layer_at(t)})
    for t in range(1, n_row):
        greet({"row": row_at(t)})

    for hops in (1, 2):
        @pl.when(col + hops < n_col)
        def _():
            greet({"col": col + hops})

        @pl.when(col - hops >= 0)
        def _():
            greet({"col": col - hops})

    def low_copy(src, s, l, sem, device):
        return pltpu.make_async_remote_copy(
            src_ref=src, dst_ref=low_all.at[s, l], send_sem=sem, recv_sem=low_recv.at[s, l],
            device_id=device, device_id_type=MESH)

    def up_copy(src, l, sem, device):
        return pltpu.make_async_remote_copy(
            src_ref=src, dst_ref=up_all.at[row, l], send_sem=sem, recv_sem=up_recv.at[row, l],
            device_id=device, device_id_type=MESH)

    def low_rows(l):
        return lower.at[pl.ds(pl.multiple_of(l * high, high), high)]

    def right(s, l, hops=1):
        sem = line_send.at[2 * hops - 2, s, l]
        return low_copy(low_all.at[s, l], s, l, sem, {"col": col + hops})

    def left(s, l, hops=1):
        sem = line_send.at[2 * hops - 1, s, l]
        return low_copy(low_all.at[s, l], s, l, sem, {"col": col - hops})

    def plane(t):
        l = layer_at(t)
        return low_copy(low_rows(l), col, lay, low_send.at[l], {"layer": l})

    def up_plane(t):
        l = layer_at(t)
        return up_copy(upper, lay, up_send.at[l], {"layer": l})

    def up_row(l, t):
        r = row_at(t)
        return up_copy(up_all.at[row, l], l, up_fwd.at[r, l], {"row": r})

    def ids_copy(which, src, dst, t):
        l = layer_at(t)
        return pltpu.make_async_remote_copy(
            src_ref=src, dst_ref=dst.at[lay], send_sem=ids_send.at[which, l],
            recv_sem=ids_recv.at[which, lay], device_id={"layer": l}, device_id_type=MESH)

    def low_arrived(s, l):
        low_copy(low_all.at[s, l], s, l, low_send.at[0], {"layer": layer_at(1)}).wait_recv()

    def leaf(i):
        per = ll.shape[0] // LEAF_ROWS
        rows = pl.ds(pl.multiple_of(lax.rem(i, per) * LEAF_ROWS, LEAF_ROWS), LEAF_ROWS)
        cols = pl.ds(pl.multiple_of((i // per) * LEAF_COLS, LEAF_COLS), LEAF_COLS)
        update = jnp.dot(ll[rows, :], lu[:, cols], preferred_element_type=jnp.float32)
        leaf_v[rows, cols] = (lf[rows, cols].astype(jnp.float32) - update).astype(leaf_v.dtype)

    n_leaf = (ll.shape[0] // LEAF_ROWS) * (lu.shape[1] // LEAF_COLS)
    place = row * n_col + col

    local[0].wait()
    local[1].wait()
    for copy in local[4:]:
        copy.start()
    lower[...] = jnp.dot(
        l_v[...], inv_u[l_ids_sm[0, place] % panels], preferred_element_type=jnp.float32
    ).astype(lower.dtype)
    low_all[col, lay] = low_rows(lay)[...]

    on_line = sum(
        (col + hops < n_col).astype(jnp.int32) + (col - hops >= 0).astype(jnp.int32)
        for hops in (1, 2))
    pl.semaphore_wait(barrier, n_layer - 1 + n_row - 1 + on_line)

    for t in range(1, n_layer):
        plane(t).start()

    def spread(l):
        for hops in (1, 2):
            @pl.when(col + hops < n_col)
            def _():
                right(col, l, hops).start()

            @pl.when(col - hops >= 0)
            def _():
                left(col, l, hops).start()

    spread(lay)

    local[2].wait()
    local[3].wait()
    upper[...] = jnp.dot(
        inv_l[u_ids_sm[0, place] // tiles_side], u_v[...], preferred_element_type=jnp.float32
    ).astype(upper.dtype)
    up_all[row, lay] = upper[...]
    for t in range(1, n_row):
        up_row(lay, t).start()
    for t in range(1, n_layer):
        l = layer_at(t)
        low_arrived(col, l)
        spread(l)
    for t in range(1, n_layer):
        up_plane(t).start()
    for t in range(1, n_layer):
        ids_copy(0, l_ids_hbm, l_ids_all, t).start()
        ids_copy(1, u_ids_hbm, u_ids_all, t).start()

    up_round = max(1, n_col - 2)
    n_steps = (n_col - 1) * n_layer
    leaf_from = min(2, n_steps - 1)

    def line_step(step, carry):
        d = step // n_layer + 1
        t = lax.rem(step, n_layer)
        l = layer_at(t)

        @pl.when(col - d >= 0)
        def _():
            low_arrived(col - d, l)

            @pl.when((d > 1) & (col + 1 < n_col))
            def _():
                right(col - d, l).start()

        @pl.when(col + d < n_col)
        def _():
            low_arrived(col + d, l)

            @pl.when((d > 1) & (col > 0))
            def _():
                left(col + d, l).start()

        @pl.when((d == up_round) & (t > 0))
        def _():
            up_copy(upper, l, up_send.at[l], {"layer": l}).wait_recv()
            for u in range(1, n_row):
                up_row(l, u).start()

        @pl.when(step == leaf_from)
        def _():
            for copy in local[4:7]:
                copy.wait()

        @pl.when((step >= leaf_from) & (step < leaf_from + n_leaf))
        def _():
            leaf(step - leaf_from)

        return carry

    lax.fori_loop(0, n_steps, line_step, 0)
    for i in range(n_steps - leaf_from, n_leaf):
        leaf(i)
    for copy in local[7:]:
        copy.wait()

    for t in range(1, n_row):
        for l in range(n_layer):
            r = row_at(t)
            pltpu.make_async_remote_copy(
                src_ref=upper, dst_ref=up_all.at[r, l], send_sem=up_fwd.at[r, l],
                recv_sem=up_recv.at[r, l], device_id={"row": r}, device_id_type=MESH).wait_recv()
            up_row(l, t).wait_send()
    for t in range(1, n_layer):
        plane(t).wait_send()
        up_plane(t).wait_send()
        l = layer_at(t)
        for which, src, dst in ((0, l_ids_hbm, l_ids_all), (1, u_ids_hbm, u_ids_all)):
            ids_copy(which, src, dst, t).wait_send()
            pltpu.make_async_remote_copy(
                src_ref=src, dst_ref=dst.at[l], send_sem=ids_send.at[which, l],
                recv_sem=ids_recv.at[which, l], device_id={"layer": l},
                device_id_type=MESH).wait_recv()
    for l in range(n_layer):
        for d, hops in [(0, 1), (0, 2)] + [(d, 1) for d in range(2, n_col)]:
            @pl.when((col - d >= 0) & (col + hops < n_col))
            def _():
                right(col - d, l, hops).wait_send()

            @pl.when((col + d < n_col) & (col - hops >= 0))
            def _():
                left(col + d, l, hops).wait_send()


def finish(
    sizes,
    l_ids, u_ids, row_order, col_order, low_all, up_all, front_v, leaf_v,
    front_out, leaf_out, acc, sem,
):
    n_layer, n_row, n_col, tiles_side, panels = sizes
    row = lax.axis_index("row")
    col = lax.axis_index("col")
    rows_owned, cols_owned = acc.shape[0], acc.shape[1]
    leaf_copy = pltpu.make_async_copy(leaf_v, leaf_out.at[0], sem.at[0])
    leaf_copy.start()
    acc[...] = front_v[...]

    def find(order, start, count, value):
        at = jnp.int32(0)
        for a in range(count):
            at = jnp.where(order[start + a] == value, jnp.int32(a), at)
        return at

    for l in range(n_layer):
        for m2 in range(n_row):
            uid = u_ids[l, 0, m2 * n_col + col]
            for m in range(n_col):
                lid = l_ids[l, 0, row * n_col + m]

                @pl.when(lid % panels == uid // tiles_side)
                def _():
                    p = find(row_order, row * rows_owned, rows_owned, lid // panels)
                    q = find(col_order, col * cols_owned, cols_owned, uid % tiles_side)
                    acc[p, q] = acc[p, q] - jnp.dot(
                        low_all[m, l], up_all[m2, l], preferred_element_type=jnp.float32)

    front_copy = pltpu.make_async_copy(acc, front_out, sem.at[1])
    front_copy.start()
    front_copy.wait()
    leaf_copy.wait()


def shards(
    sizes,
    l_blocks, l_ids, u_blocks, u_ids, inv_upper, inv_lower, row_order, col_order,
    front_in, leaf_lower, leaf_upper, leaf_front,
):
    n_layer, n_row, n_col = sizes
    tile = l_blocks.shape[-1]
    high = front_in.shape[2]
    n_ids = l_ids.shape[1]
    tiles_side = row_order.shape[0]
    bf16, i32 = jnp.bfloat16, jnp.int32
    vmem = pl.BlockSpec(memory_space=pltpu.VMEM)
    smem = pl.BlockSpec(memory_space=pltpu.SMEM)
    any_ = pl.BlockSpec(memory_space=pl.ANY)
    hbm = pl.BlockSpec(memory_space=pltpu.HBM)
    dma = pltpu.SemaphoreType.DMA
    leaf_shape = leaf_front.shape[1:]
    low_all, up_all, l_all, u_all, front_v, leaf_v = pl.pallas_call(
        functools.partial(exchange, (n_layer, n_row, n_col, tiles_side)),
        name="exchange",
        out_shape=(
            pltpu.VMEM((n_col, n_layer, high, tile), bf16),
            pltpu.VMEM((n_row, n_layer, tile, tile), bf16),
            jax.ShapeDtypeStruct((n_layer, 1, n_ids), i32),
            jax.ShapeDtypeStruct((n_layer, 1, n_ids), i32),
            pltpu.VMEM(front_in.shape, front_in.dtype),
            pltpu.VMEM(leaf_shape, bf16),
        ),
        in_specs=[smem, smem] + [hbm] * 10,
        out_specs=(vmem, vmem, any_, any_, vmem, vmem),
        scratch_shapes=[
            pltpu.VMEM((tile, tile), bf16),
            pltpu.VMEM((tile, tile), bf16),
            pltpu.VMEM(inv_upper.shape, bf16),
            pltpu.VMEM(inv_lower.shape, bf16),
            pltpu.VMEM((tile, tile), bf16),
            pltpu.VMEM((tile, tile), bf16),
            pltpu.VMEM(leaf_lower.shape[1:], bf16),
            pltpu.VMEM(leaf_upper.shape[1:], bf16),
            pltpu.VMEM(leaf_shape, bf16),
            dma((10,)),
            dma((n_col, n_layer)),
            dma((n_layer,)),
            dma((4, n_col, n_layer)),
            dma((n_row, n_layer)),
            dma((n_layer,)),
            dma((n_row, n_layer)),
            dma((2, n_layer)),
            dma((2, n_layer)),
        ],
        compiler_params=pltpu.CompilerParams(
            collective_id=0, has_side_effects=True, vmem_limit_bytes=28 * 2**20),
    )(l_ids, u_ids, *(pltpu.with_memory_space_constraint(x, pltpu.HBM) for x in (
        l_ids, u_ids, l_blocks, u_blocks, inv_upper, inv_lower, front_in, leaf_lower,
        leaf_upper, leaf_front)))
    return pl.pallas_call(
        functools.partial(finish, (n_layer, n_row, n_col, tiles_side, inv_upper.shape[0])),
        name="finish",
        out_shape=(
            jax.ShapeDtypeStruct(front_in.shape, front_in.dtype),
            jax.ShapeDtypeStruct(leaf_front.shape, bf16),
        ),
        in_specs=[smem] * 4 + [vmem] * 4,
        out_specs=(any_, any_),
        scratch_shapes=[pltpu.VMEM(front_in.shape, front_in.dtype), dma((2,))],
        compiler_params=pltpu.CompilerParams(vmem_limit_bytes=28 * 2**20),
    )(l_all, u_all, row_order, col_order, low_all, up_all, front_v, leaf_v)


def solution(mesh):
    sizes = (mesh.shape["layer"], mesh.shape["row"], mesh.shape["col"])
    leaf = P(("layer", "row", "col"), None, None)
    return jax.shard_map(
        functools.partial(shards, sizes),
        mesh=mesh,
        in_specs=(
            P("layer", ("row", "col"), None, None),
            P("layer", None),
            P("layer", ("row", "col"), None, None),
            P("layer", None),
            P(),
            P(),
            P(),
            P(),
            P("row", "col", "layer", None),
            leaf,
            leaf,
            leaf,
        ),
        out_specs=(P("row", "col", "layer", None), leaf),
        check_vma=False,
    )
```

```python
import functools

import jax
import jax.numpy as jnp
from jax import lax
from jax.experimental import pallas as pl
from jax.experimental.pallas import tpu as pltpu
from jax.sharding import PartitionSpec as P

MESH = pl.DeviceIdType.MESH
LEAF_ROWS = 512
LEAF_COLS = 256


def exchange(
    sizes,
    l_ids_sm, u_ids_sm, l_ids_hbm, u_ids_hbm, l_hbm, u_hbm, inv_u_hbm, inv_l_hbm,
    front_hbm, ll_hbm, lu_hbm, lf_hbm,
    low_all, up_all, l_ids_all, u_ids_all, front_v, leaf_v,
    l_v, u_v, inv_u, inv_l, lower, upper, ll, lu, lf,
    loc, low_recv, low_send, line_send, up_recv, up_send, up_fwd, ids_recv, ids_send,
):
    n_layer, n_row, n_col, tiles_side = sizes
    lay = lax.axis_index("layer")
    row = lax.axis_index("row")
    col = lax.axis_index("col")
    panels = inv_u.shape[0]
    high = low_all.shape[2]

    def layer_at(t):
        return lax.rem(lay + t, n_layer)

    def row_at(t):
        return lax.rem(row + t, n_row)

    local = [
        (inv_u_hbm, inv_u), (l_hbm.at[0, 0], l_v), (inv_l_hbm, inv_l), (u_hbm.at[0, 0], u_v),
        (ll_hbm.at[0], ll), (lu_hbm.at[0], lu), (lf_hbm.at[0], lf), (front_hbm, front_v),
        (l_ids_hbm, l_ids_all.at[lay]), (u_ids_hbm, u_ids_all.at[lay]),
    ]
    local = [pltpu.make_async_copy(src, dst, loc.at[i]) for i, (src, dst) in enumerate(local)]
    for copy in local[:4]:
        copy.start()

    barrier = pltpu.get_barrier_semaphore()

    def greet(device):
        pl.semaphore_signal(barrier, inc=1, device_id=device, device_id_type=MESH)

    for t in range(1, n_layer):
        greet({"layer": layer_at(t)})
    for t in range(1, n_row):
        greet({"row": row_at(t)})

    @pl.when(col + 1 < n_col)
    def _():
        greet({"col": col + 1})

    @pl.when(col > 0)
    def _():
        greet({"col": col - 1})

    def low_copy(src, s, l, sem, device):
        return pltpu.make_async_remote_copy(
            src_ref=src, dst_ref=low_all.at[s, l], send_sem=sem, recv_sem=low_recv.at[s, l],
            device_id=device, device_id_type=MESH)

    def up_copy(src, l, sem, device):
        return pltpu.make_async_remote_copy(
            src_ref=src, dst_ref=up_all.at[row, l], send_sem=sem, recv_sem=up_recv.at[row, l],
            device_id=device, device_id_type=MESH)

    def low_rows(l):
        return lower.at[pl.ds(pl.multiple_of(l * high, high), high)]

    def right(s, l):
        return low_copy(low_all.at[s, l], s, l, line_send.at[0, s, l], {"col": col + 1})

    def left(s, l):
        return low_copy(low_all.at[s, l], s, l, line_send.at[1, s, l], {"col": col - 1})

    def plane(t):
        l = layer_at(t)
        return low_copy(low_rows(l), col, lay, low_send.at[l], {"layer": l})

    def up_plane(t):
        l = layer_at(t)
        return up_copy(upper, lay, up_send.at[l], {"layer": l})

    def up_row(l, t):
        r = row_at(t)
        return up_copy(up_all.at[row, l], l, up_fwd.at[r, l], {"row": r})

    def ids_copy(which, src, dst, t):
        l = layer_at(t)
        return pltpu.make_async_remote_copy(
            src_ref=src, dst_ref=dst.at[lay], send_sem=ids_send.at[which, l],
            recv_sem=ids_recv.at[which, lay], device_id={"layer": l}, device_id_type=MESH)

    def low_arrived(s, l):
        low_copy(low_all.at[s, l], s, l, low_send.at[0], {"layer": layer_at(1)}).wait_recv()

    def leaf(i):
        per = ll.shape[0] // LEAF_ROWS
        rows = pl.ds(pl.multiple_of(lax.rem(i, per) * LEAF_ROWS, LEAF_ROWS), LEAF_ROWS)
        cols = pl.ds(pl.multiple_of((i // per) * LEAF_COLS, LEAF_COLS), LEAF_COLS)
        update = jnp.dot(ll[rows, :], lu[:, cols], preferred_element_type=jnp.float32)
        leaf_v[rows, cols] = (lf[rows, cols].astype(jnp.float32) - update).astype(leaf_v.dtype)

    n_leaf = (ll.shape[0] // LEAF_ROWS) * (lu.shape[1] // LEAF_COLS)
    place = row * n_col + col

    local[0].wait()
    local[1].wait()
    for copy in local[4:]:
        copy.start()
    lower[...] = jnp.dot(
        l_v[...], inv_u[l_ids_sm[0, place] % panels], preferred_element_type=jnp.float32
    ).astype(lower.dtype)
    low_all[col, lay] = low_rows(lay)[...]

    on_line = (col + 1 < n_col).astype(jnp.int32) + (col > 0).astype(jnp.int32)
    pl.semaphore_wait(barrier, n_layer - 1 + n_row - 1 + on_line)

    for t in range(1, n_layer):
        plane(t).start()

    def pass_on(s, l, go_right, go_left):
        if go_right:
            @pl.when(col + 1 < n_col)
            def _():
                right(s, l).start()
        if go_left:
            @pl.when(col > 0)
            def _():
                left(s, l).start()

    pass_on(col, lay, True, True)

    local[2].wait()
    local[3].wait()
    upper[...] = jnp.dot(
        inv_l[u_ids_sm[0, place] // tiles_side], u_v[...], preferred_element_type=jnp.float32
    ).astype(upper.dtype)
    up_all[row, lay] = upper[...]
    for t in range(1, n_row):
        up_row(lay, t).start()
    for t in range(1, n_layer):
        l = layer_at(t)
        low_arrived(col, l)
        pass_on(col, l, True, True)
    for t in range(1, n_layer):
        up_plane(t).start()
    for t in range(1, n_layer):
        ids_copy(0, l_ids_hbm, l_ids_all, t).start()
        ids_copy(1, u_ids_hbm, u_ids_all, t).start()

    up_round = max(1, n_col - 2)
    n_steps = (n_col - 1) * n_layer
    leaf_from = min(2, n_steps - 1)

    def line_step(step, carry):
        d = step // n_layer + 1
        t = lax.rem(step, n_layer)
        l = layer_at(t)

        @pl.when(col - d >= 0)
        def _():
            low_arrived(col - d, l)
            pass_on(col - d, l, True, False)

        @pl.when(col + d < n_col)
        def _():
            low_arrived(col + d, l)
            pass_on(col + d, l, False, True)

        @pl.when((d == up_round) & (t > 0))
        def _():
            up_copy(upper, l, up_send.at[l], {"layer": l}).wait_recv()
            for u in range(1, n_row):
                up_row(l, u).start()

        @pl.when(step == leaf_from)
        def _():
            for copy in local[4:7]:
                copy.wait()

        @pl.when((step >= leaf_from) & (step < leaf_from + n_leaf))
        def _():
            leaf(step - leaf_from)

        return carry

    lax.fori_loop(0, n_steps, line_step, 0)
    for i in range(n_steps - leaf_from, n_leaf):
        leaf(i)
    for copy in local[7:]:
        copy.wait()

    for t in range(1, n_row):
        for l in range(n_layer):
            r = row_at(t)
            pltpu.make_async_remote_copy(
                src_ref=upper, dst_ref=up_all.at[r, l], send_sem=up_fwd.at[r, l],
                recv_sem=up_recv.at[r, l], device_id={"row": r}, device_id_type=MESH).wait_recv()
            up_row(l, t).wait_send()
    for t in range(1, n_layer):
        plane(t).wait_send()
        up_plane(t).wait_send()
        l = layer_at(t)
        for which, src, dst in ((0, l_ids_hbm, l_ids_all), (1, u_ids_hbm, u_ids_all)):
            ids_copy(which, src, dst, t).wait_send()
            pltpu.make_async_remote_copy(
                src_ref=src, dst_ref=dst.at[l], send_sem=ids_send.at[which, l],
                recv_sem=ids_recv.at[which, l], device_id={"layer": l},
                device_id_type=MESH).wait_recv()
    for d in range(n_col):
        for l in range(n_layer):
            @pl.when((col - d >= 0) & (col + 1 < n_col))
            def _():
                right(col - d, l).wait_send()

            @pl.when((col + d < n_col) & (col > 0))
            def _():
                left(col + d, l).wait_send()


def finish(
    sizes,
    l_ids, u_ids, row_order, col_order, low_all, up_all, front_v, leaf_v,
    front_out, leaf_out, acc, sem,
):
    n_layer, n_row, n_col, tiles_side, panels = sizes
    row = lax.axis_index("row")
    col = lax.axis_index("col")
    rows_owned, cols_owned = acc.shape[0], acc.shape[1]
    leaf_copy = pltpu.make_async_copy(leaf_v, leaf_out.at[0], sem.at[0])
    leaf_copy.start()

    def find(order, start, count, value):
        at = jnp.int32(0)
        for a in range(count):
            at = jnp.where(order[start + a] == value, jnp.int32(a), at)
        return at

    for l in range(n_layer):
        for m2 in range(n_row):
            uid = u_ids[l, 0, m2 * n_col + col]
            for m in range(n_col):
                lid = l_ids[l, 0, row * n_col + m]

                @pl.when(lid % panels == uid // tiles_side)
                def _():
                    p = find(row_order, row * rows_owned, rows_owned, lid // panels)
                    q = find(col_order, col * cols_owned, cols_owned, uid % tiles_side)
                    acc[p, q] = acc[p, q] - jnp.dot(
                        low_all[m, l], up_all[m2, l], preferred_element_type=jnp.float32)

    front_copy = pltpu.make_async_copy(acc, front_out, sem.at[1])
    front_copy.start()
    front_copy.wait()
    leaf_copy.wait()


def shards(
    sizes,
    l_blocks, l_ids, u_blocks, u_ids, inv_upper, inv_lower, row_order, col_order,
    front_in, leaf_lower, leaf_upper, leaf_front,
):
    n_layer, n_row, n_col = sizes
    tile = l_blocks.shape[-1]
    high = front_in.shape[2]
    n_ids = l_ids.shape[1]
    tiles_side = row_order.shape[0]
    bf16, i32 = jnp.bfloat16, jnp.int32
    vmem = pl.BlockSpec(memory_space=pltpu.VMEM)
    smem = pl.BlockSpec(memory_space=pltpu.SMEM)
    any_ = pl.BlockSpec(memory_space=pl.ANY)
    hbm = pl.BlockSpec(memory_space=pltpu.HBM)
    dma = pltpu.SemaphoreType.DMA
    leaf_shape = leaf_front.shape[1:]
    low_all, up_all, l_all, u_all, front_v, leaf_v = pl.pallas_call(
        functools.partial(exchange, (n_layer, n_row, n_col, tiles_side)),
        name="exchange",
        out_shape=(
            pltpu.VMEM((n_col, n_layer, high, tile), bf16),
            pltpu.VMEM((n_row, n_layer, tile, tile), bf16),
            jax.ShapeDtypeStruct((n_layer, 1, n_ids), i32),
            jax.ShapeDtypeStruct((n_layer, 1, n_ids), i32),
            pltpu.VMEM(front_in.shape, front_in.dtype),
            pltpu.VMEM(leaf_shape, bf16),
        ),
        in_specs=[smem, smem] + [hbm] * 10,
        out_specs=(vmem, vmem, any_, any_, vmem, vmem),
        scratch_shapes=[
            pltpu.VMEM((tile, tile), bf16),
            pltpu.VMEM((tile, tile), bf16),
            pltpu.VMEM(inv_upper.shape, bf16),
            pltpu.VMEM(inv_lower.shape, bf16),
            pltpu.VMEM((tile, tile), bf16),
            pltpu.VMEM((tile, tile), bf16),
            pltpu.VMEM(leaf_lower.shape[1:], bf16),
            pltpu.VMEM(leaf_upper.shape[1:], bf16),
            pltpu.VMEM(leaf_shape, bf16),
            dma((10,)),
            dma((n_col, n_layer)),
            dma((n_layer,)),
            dma((2, n_col, n_layer)),
            dma((n_row, n_layer)),
            dma((n_layer,)),
            dma((n_row, n_layer)),
            dma((2, n_layer)),
            dma((2, n_layer)),
        ],
        compiler_params=pltpu.CompilerParams(
            collective_id=0, has_side_effects=True, vmem_limit_bytes=28 * 2**20),
    )(l_ids, u_ids, *(pltpu.with_memory_space_constraint(x, pltpu.HBM) for x in (
        l_ids, u_ids, l_blocks, u_blocks, inv_upper, inv_lower, front_in, leaf_lower,
        leaf_upper, leaf_front)))
    return pl.pallas_call(
        functools.partial(finish, (n_layer, n_row, n_col, tiles_side, inv_upper.shape[0])),
        name="finish",
        out_shape=(
            jax.ShapeDtypeStruct(front_in.shape, front_in.dtype),
            jax.ShapeDtypeStruct(leaf_front.shape, bf16),
            pltpu.VMEM(front_in.shape, front_in.dtype),
        ),
        in_specs=[smem] * 4 + [vmem] * 4,
        out_specs=(any_, any_, vmem),
        scratch_shapes=[dma((2,))],
        input_output_aliases={6: 2},
        compiler_params=pltpu.CompilerParams(vmem_limit_bytes=28 * 2**20),
    )(l_all, u_all, row_order, col_order, low_all, up_all, front_v, leaf_v)[:2]


def solution(mesh):
    sizes = (mesh.shape["layer"], mesh.shape["row"], mesh.shape["col"])
    leaf = P(("layer", "row", "col"), None, None)
    return jax.shard_map(
        functools.partial(shards, sizes),
        mesh=mesh,
        in_specs=(
            P("layer", ("row", "col"), None, None),
            P("layer", None),
            P("layer", ("row", "col"), None, None),
            P("layer", None),
            P(),
            P(),
            P(),
            P(),
            P("row", "col", "layer", None),
            leaf,
            leaf,
            leaf,
        ),
        out_specs=(P("row", "col", "layer", None), leaf),
        check_vma=False,
    )
```

```python
import functools

import jax
import jax.numpy as jnp
from jax import lax
from jax.experimental import pallas as pl
from jax.experimental.pallas import tpu as pltpu
from jax.sharding import PartitionSpec as P

MESH = pl.DeviceIdType.MESH
LEAF_ROWS = 512
LEAF_COLS = 256


def exchange(
    sizes,
    l_ids_sm, u_ids_sm, l_ids_hbm, u_ids_hbm, l_hbm, u_hbm, inv_u_hbm, inv_l_hbm,
    front_hbm, ll_hbm, lu_hbm, lf_hbm,
    low_all, up_all, l_ids_all, u_ids_all, front_v, leaf_v,
    l_v, u_v, inv_u, inv_l, lower, upper, ll, lu, lf,
    loc, low_recv, low_send, line_send, up_recv, up_send, up_fwd, ids_recv, ids_send,
):
    n_layer, n_row, n_col, tiles_side = sizes
    lay = lax.axis_index("layer")
    row = lax.axis_index("row")
    col = lax.axis_index("col")
    panels = inv_u.shape[0]
    high = low_all.shape[2]

    def layer_at(t):
        return lax.rem(lay + t, n_layer)

    def row_at(t):
        return lax.rem(row + t, n_row)

    local = [
        (inv_u_hbm, inv_u), (l_hbm.at[0, 0], l_v), (inv_l_hbm, inv_l), (u_hbm.at[0, 0], u_v),
        (ll_hbm.at[0], ll), (lu_hbm.at[0], lu), (lf_hbm.at[0], lf), (front_hbm, front_v),
        (l_ids_hbm, l_ids_all.at[lay]), (u_ids_hbm, u_ids_all.at[lay]),
    ]
    local = [pltpu.make_async_copy(src, dst, loc.at[i]) for i, (src, dst) in enumerate(local)]
    barrier = pltpu.get_barrier_semaphore()

    def greet(device):
        pl.semaphore_signal(barrier, inc=1, device_id=device, device_id_type=MESH)

    for t in range(1, n_layer):
        greet({"layer": layer_at(t)})
    for t in range(1, n_row):
        greet({"row": row_at(t)})

    @pl.when(col + 1 < n_col)
    def _():
        greet({"col": col + 1})

    @pl.when(col > 0)
    def _():
        greet({"col": col - 1})

    for copy in local[:2]:
        copy.start()

    def low_copy(src, s, l, sem, device):
        return pltpu.make_async_remote_copy(
            src_ref=src, dst_ref=low_all.at[s, l], send_sem=sem, recv_sem=low_recv.at[s, l],
            device_id=device, device_id_type=MESH)

    def up_copy(src, l, sem, device):
        return pltpu.make_async_remote_copy(
            src_ref=src, dst_ref=up_all.at[row, l], send_sem=sem, recv_sem=up_recv.at[row, l],
            device_id=device, device_id_type=MESH)

    def low_rows(l):
        return lower.at[pl.ds(pl.multiple_of(l * high, high), high)]

    def right(s, l):
        return low_copy(low_all.at[s, l], s, l, line_send.at[0, s, l], {"col": col + 1})

    def left(s, l):
        return low_copy(low_all.at[s, l], s, l, line_send.at[1, s, l], {"col": col - 1})

    def plane(t):
        l = layer_at(t)
        return low_copy(low_rows(l), col, lay, low_send.at[l], {"layer": l})

    def up_plane(t):
        l = layer_at(t)
        return up_copy(upper, lay, up_send.at[l], {"layer": l})

    def up_row(l, t):
        r = row_at(t)
        return up_copy(up_all.at[row, l], l, up_fwd.at[r, l], {"row": r})

    def ids_copy(which, src, dst, t):
        l = layer_at(t)
        return pltpu.make_async_remote_copy(
            src_ref=src, dst_ref=dst.at[lay], send_sem=ids_send.at[which, l],
            recv_sem=ids_recv.at[which, lay], device_id={"layer": l}, device_id_type=MESH)

    def low_arrived(s, l):
        low_copy(low_all.at[s, l], s, l, low_send.at[0], {"layer": layer_at(1)}).wait_recv()

    def leaf(i):
        per = ll.shape[0] // LEAF_ROWS
        rows = pl.ds(pl.multiple_of(lax.rem(i, per) * LEAF_ROWS, LEAF_ROWS), LEAF_ROWS)
        cols = pl.ds(pl.multiple_of((i // per) * LEAF_COLS, LEAF_COLS), LEAF_COLS)
        update = jnp.dot(ll[rows, :], lu[:, cols], preferred_element_type=jnp.float32)
        leaf_v[rows, cols] = (lf[rows, cols].astype(jnp.float32) - update).astype(leaf_v.dtype)

    n_leaf = (ll.shape[0] // LEAF_ROWS) * (lu.shape[1] // LEAF_COLS)
    place = row * n_col + col

    local[0].wait()
    local[1].wait()
    for copy in local[2:4]:
        copy.start()
    lower[...] = jnp.dot(
        l_v[...], inv_u[l_ids_sm[0, place] % panels], preferred_element_type=jnp.float32
    ).astype(lower.dtype)
    low_all[col, lay] = low_rows(lay)[...]

    on_line = (col + 1 < n_col).astype(jnp.int32) + (col > 0).astype(jnp.int32)
    pl.semaphore_wait(barrier, n_layer - 1 + n_row - 1 + on_line)

    for t in range(1, n_layer):
        plane(t).start()

    def pass_on(s, l, go_right, go_left):
        if go_right:
            @pl.when(col + 1 < n_col)
            def _():
                right(s, l).start()
        if go_left:
            @pl.when(col > 0)
            def _():
                left(s, l).start()

    pass_on(col, lay, True, True)

    local[2].wait()
    local[3].wait()
    for copy in local[4:]:
        copy.start()
    upper[...] = jnp.dot(
        inv_l[u_ids_sm[0, place] // tiles_side], u_v[...], preferred_element_type=jnp.float32
    ).astype(upper.dtype)
    up_all[row, lay] = upper[...]
    for t in range(1, n_row):
        up_row(lay, t).start()
    for t in range(1, n_layer):
        l = layer_at(t)
        low_arrived(col, l)
        pass_on(col, l, True, True)
    for t in range(1, n_layer):
        up_plane(t).start()
    for t in range(1, n_layer):
        ids_copy(0, l_ids_hbm, l_ids_all, t).start()
        ids_copy(1, u_ids_hbm, u_ids_all, t).start()

    inner = (col > 0) & (col + 1 < n_col)
    up_round = jnp.where(inner, n_col - 1, max(1, n_col - 2))
    n_steps = (n_col - 1) * n_layer
    leaf_from = min(2, n_steps - 1)

    def line_step(step, carry):
        d = step // n_layer + 1
        t = lax.rem(step, n_layer)
        l = layer_at(t)

        @pl.when(col - d >= 0)
        def _():
            low_arrived(col - d, l)
            pass_on(col - d, l, True, False)

        @pl.when(col + d < n_col)
        def _():
            low_arrived(col + d, l)
            pass_on(col + d, l, False, True)

        @pl.when((d == up_round) & (t > 0))
        def _():
            up_copy(upper, l, up_send.at[l], {"layer": l}).wait_recv()
            for u in range(1, n_row):
                up_row(l, u).start()

        @pl.when(step == leaf_from)
        def _():
            for copy in local[4:7]:
                copy.wait()

        @pl.when((step >= leaf_from) & (step < leaf_from + n_leaf))
        def _():
            leaf(step - leaf_from)

        return carry

    lax.fori_loop(0, n_steps, line_step, 0)
    for i in range(n_steps - leaf_from, n_leaf):
        leaf(i)
    for copy in local[7:]:
        copy.wait()

    for t in range(1, n_row):
        for l in range(n_layer):
            r = row_at(t)
            pltpu.make_async_remote_copy(
                src_ref=upper, dst_ref=up_all.at[r, l], send_sem=up_fwd.at[r, l],
                recv_sem=up_recv.at[r, l], device_id={"row": r}, device_id_type=MESH).wait_recv()
            up_row(l, t).wait_send()
    for t in range(1, n_layer):
        plane(t).wait_send()
        up_plane(t).wait_send()
        l = layer_at(t)
        for which, src, dst in ((0, l_ids_hbm, l_ids_all), (1, u_ids_hbm, u_ids_all)):
            ids_copy(which, src, dst, t).wait_send()
            pltpu.make_async_remote_copy(
                src_ref=src, dst_ref=dst.at[l], send_sem=ids_send.at[which, l],
                recv_sem=ids_recv.at[which, l], device_id={"layer": l},
                device_id_type=MESH).wait_recv()
    for d in range(n_col):
        for l in range(n_layer):
            @pl.when((col - d >= 0) & (col + 1 < n_col))
            def _():
                right(col - d, l).wait_send()

            @pl.when((col + d < n_col) & (col > 0))
            def _():
                left(col + d, l).wait_send()


def finish(
    sizes,
    l_ids, u_ids, row_order, col_order, low_all, up_all, front_v, leaf_v,
    front_out, leaf_out, acc, sem,
):
    n_layer, n_row, n_col, tiles_side, panels = sizes
    row = lax.axis_index("row")
    col = lax.axis_index("col")
    rows_owned, cols_owned = acc.shape[0], acc.shape[1]
    leaf_copy = pltpu.make_async_copy(leaf_v, leaf_out.at[0], sem.at[0])
    leaf_copy.start()

    def find(order, start, count, value):
        at = jnp.int32(0)
        for a in range(count):
            at = jnp.where(order[start + a] == value, jnp.int32(a), at)
        return at

    for l in range(n_layer):
        for m2 in range(n_row):
            uid = u_ids[l, 0, m2 * n_col + col]
            for m in range(n_col):
                lid = l_ids[l, 0, row * n_col + m]

                @pl.when(lid % panels == uid // tiles_side)
                def _():
                    p = find(row_order, row * rows_owned, rows_owned, lid // panels)
                    q = find(col_order, col * cols_owned, cols_owned, uid % tiles_side)
                    acc[p, q] = acc[p, q] - jnp.dot(
                        low_all[m, l], up_all[m2, l], preferred_element_type=jnp.float32)

    front_copy = pltpu.make_async_copy(acc, front_out, sem.at[1])
    front_copy.start()
    front_copy.wait()
    leaf_copy.wait()


def shards(
    sizes,
    l_blocks, l_ids, u_blocks, u_ids, inv_upper, inv_lower, row_order, col_order,
    front_in, leaf_lower, leaf_upper, leaf_front,
):
    n_layer, n_row, n_col = sizes
    tile = l_blocks.shape[-1]
    high = front_in.shape[2]
    n_ids = l_ids.shape[1]
    tiles_side = row_order.shape[0]
    bf16, i32 = jnp.bfloat16, jnp.int32
    vmem = pl.BlockSpec(memory_space=pltpu.VMEM)
    smem = pl.BlockSpec(memory_space=pltpu.SMEM)
    any_ = pl.BlockSpec(memory_space=pl.ANY)
    hbm = pl.BlockSpec(memory_space=pltpu.HBM)
    dma = pltpu.SemaphoreType.DMA
    leaf_shape = leaf_front.shape[1:]
    low_all, up_all, l_all, u_all, front_v, leaf_v = pl.pallas_call(
        functools.partial(exchange, (n_layer, n_row, n_col, tiles_side)),
        name="exchange",
        out_shape=(
            pltpu.VMEM((n_col, n_layer, high, tile), bf16),
            pltpu.VMEM((n_row, n_layer, tile, tile), bf16),
            jax.ShapeDtypeStruct((n_layer, 1, n_ids), i32),
            jax.ShapeDtypeStruct((n_layer, 1, n_ids), i32),
            pltpu.VMEM(front_in.shape, front_in.dtype),
            pltpu.VMEM(leaf_shape, bf16),
        ),
        in_specs=[smem, smem] + [hbm] * 10,
        out_specs=(vmem, vmem, any_, any_, vmem, vmem),
        scratch_shapes=[
            pltpu.VMEM((tile, tile), bf16),
            pltpu.VMEM((tile, tile), bf16),
            pltpu.VMEM(inv_upper.shape, bf16),
            pltpu.VMEM(inv_lower.shape, bf16),
            pltpu.VMEM((tile, tile), bf16),
            pltpu.VMEM((tile, tile), bf16),
            pltpu.VMEM(leaf_lower.shape[1:], bf16),
            pltpu.VMEM(leaf_upper.shape[1:], bf16),
            pltpu.VMEM(leaf_shape, bf16),
            dma((10,)),
            dma((n_col, n_layer)),
            dma((n_layer,)),
            dma((2, n_col, n_layer)),
            dma((n_row, n_layer)),
            dma((n_layer,)),
            dma((n_row, n_layer)),
            dma((2, n_layer)),
            dma((2, n_layer)),
        ],
        compiler_params=pltpu.CompilerParams(
            collective_id=0, has_side_effects=True, vmem_limit_bytes=28 * 2**20),
    )(l_ids, u_ids, *(pltpu.with_memory_space_constraint(x, pltpu.HBM) for x in (
        l_ids, u_ids, l_blocks, u_blocks, inv_upper, inv_lower, front_in, leaf_lower,
        leaf_upper, leaf_front)))
    return pl.pallas_call(
        functools.partial(finish, (n_layer, n_row, n_col, tiles_side, inv_upper.shape[0])),
        name="finish",
        out_shape=(
            jax.ShapeDtypeStruct(front_in.shape, front_in.dtype),
            jax.ShapeDtypeStruct(leaf_front.shape, bf16),
            pltpu.VMEM(front_in.shape, front_in.dtype),
        ),
        in_specs=[smem] * 4 + [vmem] * 4,
        out_specs=(any_, any_, vmem),
        scratch_shapes=[dma((2,))],
        input_output_aliases={6: 2},
        compiler_params=pltpu.CompilerParams(vmem_limit_bytes=28 * 2**20),
    )(l_all, u_all, row_order, col_order, low_all, up_all, front_v, leaf_v)[:2]


def solution(mesh):
    sizes = (mesh.shape["layer"], mesh.shape["row"], mesh.shape["col"])
    leaf = P(("layer", "row", "col"), None, None)
    return jax.shard_map(
        functools.partial(shards, sizes),
        mesh=mesh,
        in_specs=(
            P("layer", ("row", "col"), None, None),
            P("layer", None),
            P("layer", ("row", "col"), None, None),
            P("layer", None),
            P(),
            P(),
            P(),
            P(),
            P("row", "col", "layer", None),
            leaf,
            leaf,
            leaf,
        ),
        out_specs=(P("row", "col", "layer", None), leaf),
        check_vma=False,
    )
```

```python
import functools

import jax
import jax.numpy as jnp
from jax import lax
from jax.experimental import pallas as pl
from jax.experimental.pallas import tpu as pltpu
from jax.sharding import PartitionSpec as P

MESH = pl.DeviceIdType.MESH
LEAF_ROWS = 512
LEAF_COLS = 256


def exchange(
    sizes,
    l_ids_sm, u_ids_sm, l_ids_hbm, u_ids_hbm, l_hbm, u_hbm, inv_u_hbm, inv_l_hbm,
    front_hbm, ll_hbm, lu_hbm, lf_hbm,
    low_all, up_all, l_ids_all, u_ids_all, front_v, leaf_v,
    l_v, u_v, inv_u, inv_l, lower, upper, ll, lu, lf,
    loc, low_recv, low_send, line_send, up_recv, up_send, up_fwd, ids_recv, ids_send,
):
    n_layer, n_row, n_col, tiles_side = sizes
    lay = lax.axis_index("layer")
    row = lax.axis_index("row")
    col = lax.axis_index("col")
    panels = inv_u.shape[0]
    high = low_all.shape[2]

    def layer_at(t):
        return lax.rem(lay + t, n_layer)

    def row_at(t):
        return lax.rem(row + t, n_row)

    local = [
        (inv_u_hbm, inv_u), (l_hbm.at[0, 0], l_v), (inv_l_hbm, inv_l), (u_hbm.at[0, 0], u_v),
        (ll_hbm.at[0], ll), (lu_hbm.at[0], lu), (lf_hbm.at[0], lf), (front_hbm, front_v),
        (l_ids_hbm, l_ids_all.at[lay]), (u_ids_hbm, u_ids_all.at[lay]),
    ]
    local = [pltpu.make_async_copy(src, dst, loc.at[i]) for i, (src, dst) in enumerate(local)]
    barrier = pltpu.get_barrier_semaphore()

    def greet(device):
        pl.semaphore_signal(barrier, inc=1, device_id=device, device_id_type=MESH)

    for t in range(1, n_layer):
        greet({"layer": layer_at(t)})
    for t in range(1, n_row):
        greet({"row": row_at(t)})

    @pl.when(col + 1 < n_col)
    def _():
        greet({"col": col + 1})

    @pl.when(col > 0)
    def _():
        greet({"col": col - 1})

    for copy in local[:2]:
        copy.start()

    def low_copy(src, s, l, sem, device):
        return pltpu.make_async_remote_copy(
            src_ref=src, dst_ref=low_all.at[s, l], send_sem=sem, recv_sem=low_recv.at[s, l],
            device_id=device, device_id_type=MESH)

    def up_copy(src, l, sem, device):
        return pltpu.make_async_remote_copy(
            src_ref=src, dst_ref=up_all.at[row, l], send_sem=sem, recv_sem=up_recv.at[row, l],
            device_id=device, device_id_type=MESH)

    def low_rows(l):
        return lower.at[pl.ds(pl.multiple_of(l * high, high), high)]

    def right(s, l):
        return low_copy(low_all.at[s, l], s, l, line_send.at[0, s, l], {"col": col + 1})

    def left(s, l):
        return low_copy(low_all.at[s, l], s, l, line_send.at[1, s, l], {"col": col - 1})

    def plane(t):
        l = layer_at(t)
        return low_copy(low_rows(l), col, lay, low_send.at[l], {"layer": l})

    def up_plane(t):
        l = layer_at(t)
        return up_copy(upper, lay, up_send.at[l], {"layer": l})

    def up_row(l, t):
        r = row_at(t)
        return up_copy(up_all.at[row, l], l, up_fwd.at[r, l], {"row": r})

    def ids_copy(which, src, dst, t):
        l = layer_at(t)
        return pltpu.make_async_remote_copy(
            src_ref=src, dst_ref=dst.at[lay], send_sem=ids_send.at[which, l],
            recv_sem=ids_recv.at[which, lay], device_id={"layer": l}, device_id_type=MESH)

    def low_arrived(s, l):
        low_copy(low_all.at[s, l], s, l, low_send.at[0], {"layer": layer_at(1)}).wait_recv()

    def leaf(i):
        per = ll.shape[0] // LEAF_ROWS
        rows = pl.ds(pl.multiple_of(lax.rem(i, per) * LEAF_ROWS, LEAF_ROWS), LEAF_ROWS)
        cols = pl.ds(pl.multiple_of((i // per) * LEAF_COLS, LEAF_COLS), LEAF_COLS)
        update = jnp.dot(ll[rows, :], lu[:, cols], preferred_element_type=jnp.float32)
        leaf_v[rows, cols] = (lf[rows, cols].astype(jnp.float32) - update).astype(leaf_v.dtype)

    n_leaf = (ll.shape[0] // LEAF_ROWS) * (lu.shape[1] // LEAF_COLS)
    place = row * n_col + col

    local[0].wait()
    local[1].wait()
    for copy in local[2:4]:
        copy.start()
    lower[...] = jnp.dot(
        l_v[...], inv_u[l_ids_sm[0, place] % panels], preferred_element_type=jnp.float32
    ).astype(lower.dtype)
    low_all[col, lay] = low_rows(lay)[...]

    on_line = (col + 1 < n_col).astype(jnp.int32) + (col > 0).astype(jnp.int32)
    pl.semaphore_wait(barrier, n_layer - 1 + n_row - 1 + on_line)

    for t in range(1, n_layer):
        plane(t).start()

    def pass_on(s, l, go_right, go_left):
        if go_right:
            @pl.when(col + 1 < n_col)
            def _():
                right(s, l).start()
        if go_left:
            @pl.when(col > 0)
            def _():
                left(s, l).start()

    pass_on(col, lay, True, True)

    local[2].wait()
    local[3].wait()
    for copy in local[4:]:
        copy.start()
    upper[...] = jnp.dot(
        inv_l[u_ids_sm[0, place] // tiles_side], u_v[...], preferred_element_type=jnp.float32
    ).astype(upper.dtype)
    up_all[row, lay] = upper[...]
    for t in range(1, n_row):
        up_row(lay, t).start()
    for t in range(1, n_layer):
        l = layer_at(t)
        low_arrived(col, l)
        pass_on(col, l, True, True)
    for t in range(1, n_layer):
        up_plane(t).start()
    for t in range(1, n_layer):
        ids_copy(0, l_ids_hbm, l_ids_all, t).start()
        ids_copy(1, u_ids_hbm, u_ids_all, t).start()

    inner = (col > 0) & (col + 1 < n_col)
    up_round = jnp.where(inner, n_col - 1, max(1, n_col - 2))
    n_steps = (n_col - 1) * n_layer
    leaf_from = min(2, n_steps - 1)

    def line_step(step, carry):
        d = step // n_layer + 1
        t = lax.rem(step, n_layer)
        l = layer_at(t)

        @pl.when((d == up_round) & (t < n_layer - 1))
        def _():
            peer = layer_at(t + 1)
            up_copy(upper, peer, up_send.at[peer], {"layer": peer}).wait_recv()
            for u in range(1, n_row):
                up_row(peer, u).start()

        @pl.when(col - d >= 0)
        def _():
            low_arrived(col - d, l)
            pass_on(col - d, l, True, False)

        @pl.when(col + d < n_col)
        def _():
            low_arrived(col + d, l)
            pass_on(col + d, l, False, True)

        @pl.when(step == leaf_from)
        def _():
            for copy in local[4:7]:
                copy.wait()

        @pl.when((step >= leaf_from) & (step < leaf_from + n_leaf))
        def _():
            leaf(step - leaf_from)

        return carry

    lax.fori_loop(0, n_steps, line_step, 0)
    for i in range(n_steps - leaf_from, n_leaf):
        leaf(i)
    for copy in local[7:]:
        copy.wait()

    for t in range(1, n_row):
        for l in range(n_layer):
            r = row_at(t)
            pltpu.make_async_remote_copy(
                src_ref=upper, dst_ref=up_all.at[r, l], send_sem=up_fwd.at[r, l],
                recv_sem=up_recv.at[r, l], device_id={"row": r}, device_id_type=MESH).wait_recv()
            up_row(l, t).wait_send()
    for t in range(1, n_layer):
        plane(t).wait_send()
        up_plane(t).wait_send()
        l = layer_at(t)
        for which, src, dst in ((0, l_ids_hbm, l_ids_all), (1, u_ids_hbm, u_ids_all)):
            ids_copy(which, src, dst, t).wait_send()
            pltpu.make_async_remote_copy(
                src_ref=src, dst_ref=dst.at[l], send_sem=ids_send.at[which, l],
                recv_sem=ids_recv.at[which, l], device_id={"layer": l},
                device_id_type=MESH).wait_recv()
    for d in range(n_col):
        for l in range(n_layer):
            @pl.when((col - d >= 0) & (col + 1 < n_col))
            def _():
                right(col - d, l).wait_send()

            @pl.when((col + d < n_col) & (col > 0))
            def _():
                left(col + d, l).wait_send()


def finish(
    sizes,
    l_ids, u_ids, row_order, col_order, low_all, up_all, front_v, leaf_v,
    front_out, leaf_out, acc, sem,
):
    n_layer, n_row, n_col, tiles_side, panels = sizes
    row = lax.axis_index("row")
    col = lax.axis_index("col")
    rows_owned, cols_owned = acc.shape[0], acc.shape[1]
    leaf_copy = pltpu.make_async_copy(leaf_v, leaf_out.at[0], sem.at[0])
    leaf_copy.start()

    def find(order, start, count, value):
        at = jnp.int32(0)
        for a in range(count):
            at = jnp.where(order[start + a] == value, jnp.int32(a), at)
        return at

    for l in range(n_layer):
        for m2 in range(n_row):
            uid = u_ids[l, 0, m2 * n_col + col]
            for m in range(n_col):
                lid = l_ids[l, 0, row * n_col + m]

                @pl.when(lid % panels == uid // tiles_side)
                def _():
                    p = find(row_order, row * rows_owned, rows_owned, lid // panels)
                    q = find(col_order, col * cols_owned, cols_owned, uid % tiles_side)
                    acc[p, q] = acc[p, q] - jnp.dot(
                        low_all[m, l], up_all[m2, l], preferred_element_type=jnp.float32)

    front_copy = pltpu.make_async_copy(acc, front_out, sem.at[1])
    front_copy.start()
    front_copy.wait()
    leaf_copy.wait()


def shards(
    sizes,
    l_blocks, l_ids, u_blocks, u_ids, inv_upper, inv_lower, row_order, col_order,
    front_in, leaf_lower, leaf_upper, leaf_front,
):
    n_layer, n_row, n_col = sizes
    tile = l_blocks.shape[-1]
    high = front_in.shape[2]
    n_ids = l_ids.shape[1]
    tiles_side = row_order.shape[0]
    bf16, i32 = jnp.bfloat16, jnp.int32
    vmem = pl.BlockSpec(memory_space=pltpu.VMEM)
    smem = pl.BlockSpec(memory_space=pltpu.SMEM)
    any_ = pl.BlockSpec(memory_space=pl.ANY)
    hbm = pl.BlockSpec(memory_space=pltpu.HBM)
    dma = pltpu.SemaphoreType.DMA
    leaf_shape = leaf_front.shape[1:]
    low_all, up_all, l_all, u_all, front_v, leaf_v = pl.pallas_call(
        functools.partial(exchange, (n_layer, n_row, n_col, tiles_side)),
        name="exchange",
        out_shape=(
            pltpu.VMEM((n_col, n_layer, high, tile), bf16),
            pltpu.VMEM((n_row, n_layer, tile, tile), bf16),
            jax.ShapeDtypeStruct((n_layer, 1, n_ids), i32),
            jax.ShapeDtypeStruct((n_layer, 1, n_ids), i32),
            pltpu.VMEM(front_in.shape, front_in.dtype),
            pltpu.VMEM(leaf_shape, bf16),
        ),
        in_specs=[smem, smem] + [hbm] * 10,
        out_specs=(vmem, vmem, any_, any_, vmem, vmem),
        scratch_shapes=[
            pltpu.VMEM((tile, tile), bf16),
            pltpu.VMEM((tile, tile), bf16),
            pltpu.VMEM(inv_upper.shape, bf16),
            pltpu.VMEM(inv_lower.shape, bf16),
            pltpu.VMEM((tile, tile), bf16),
            pltpu.VMEM((tile, tile), bf16),
            pltpu.VMEM(leaf_lower.shape[1:], bf16),
            pltpu.VMEM(leaf_upper.shape[1:], bf16),
            pltpu.VMEM(leaf_shape, bf16),
            dma((10,)),
            dma((n_col, n_layer)),
            dma((n_layer,)),
            dma((2, n_col, n_layer)),
            dma((n_row, n_layer)),
            dma((n_layer,)),
            dma((n_row, n_layer)),
            dma((2, n_layer)),
            dma((2, n_layer)),
        ],
        compiler_params=pltpu.CompilerParams(
            collective_id=0, has_side_effects=True, vmem_limit_bytes=28 * 2**20),
    )(l_ids, u_ids, *(pltpu.with_memory_space_constraint(x, pltpu.HBM) for x in (
        l_ids, u_ids, l_blocks, u_blocks, inv_upper, inv_lower, front_in, leaf_lower,
        leaf_upper, leaf_front)))
    return pl.pallas_call(
        functools.partial(finish, (n_layer, n_row, n_col, tiles_side, inv_upper.shape[0])),
        name="finish",
        out_shape=(
            jax.ShapeDtypeStruct(front_in.shape, front_in.dtype),
            jax.ShapeDtypeStruct(leaf_front.shape, bf16),
            pltpu.VMEM(front_in.shape, front_in.dtype),
        ),
        in_specs=[smem] * 4 + [vmem] * 4,
        out_specs=(any_, any_, vmem),
        scratch_shapes=[dma((2,))],
        input_output_aliases={6: 2},
        compiler_params=pltpu.CompilerParams(vmem_limit_bytes=28 * 2**20),
    )(l_all, u_all, row_order, col_order, low_all, up_all, front_v, leaf_v)[:2]


def solution(mesh):
    sizes = (mesh.shape["layer"], mesh.shape["row"], mesh.shape["col"])
    leaf = P(("layer", "row", "col"), None, None)
    return jax.shard_map(
        functools.partial(shards, sizes),
        mesh=mesh,
        in_specs=(
            P("layer", ("row", "col"), None, None),
            P("layer", None),
            P("layer", ("row", "col"), None, None),
            P("layer", None),
            P(),
            P(),
            P(),
            P(),
            P("row", "col", "layer", None),
            leaf,
            leaf,
            leaf,
        ),
        out_specs=(P("row", "col", "layer", None), leaf),
        check_vma=False,
    )
```
